32 devices in a mesh: rows: 8 (over y, x, core), batch: 4 (over z).
Axes of the slice: x: 2, y: 2, z: 4, core: 2. Of those that a mesh axis runs over, the one named last changes fastest.
Arguments:
- bases: bfloat16 [24576, 1024], P('rows', 'batch'), may hold values from -30 to 30
- start: float32 [1024, 512], P('batch'), may hold values from -6 to 6
Outputs:
- modes: bfloat16 [24576, 512], P(('rows', 'batch'))
The draws below stay inside these ranges and needn't reach their ends.
All inputs are finite; a program needn't handle non-finite values.
Results may differ from the reference program's by a relative error of at most 0.0041.
Values may be sent and summed in bfloat16 or wider, within the bound.
No kernel may reach another device: no remote copies, remote signals or barrier semaphores. Data moves between devices by JAX's collectives and lax.ppermute only.
A program may use at most 128 MiB of HBM per device.

```python
import math
import jax
import jax.numpy as jnp
from jax import lax

R = 256
M = 512
ITERS = 2
ROWS_DEV = 3072
COLS = 1024
ROWS = 24576


def draw_bases(key, part):
    base_key = jax.random.fold_in(key, 17)
    keys = jax.random.split(base_key, 4)
    row_pos = jnp.arange(ROWS, dtype=jnp.float32) / ROWS
    shared = jax.random.truncated_normal(keys[0], -4.0, 4.0, (ROWS, R), jnp.float32)
    own_part = jax.random.truncated_normal(keys[1], -4.0, 4.0, (ROWS, COLS), jnp.float32)
    row_scale = jnp.exp(jax.random.uniform(keys[2], (ROWS,), jnp.float32, math.log(0.3), math.log(3.0)) + 0.55 * row_pos)
    shared_weight = 0.5
    own_weight = 0.65
    col_scale = jnp.exp(jax.random.uniform(keys[3], (COLS,), jnp.float32, math.log(0.6), math.log(1.8)))
    mixed = shared_weight * jnp.tile(shared, (1, COLS // R)) + own_weight * own_part
    return (0.5 * mixed * row_scale[:, None] * col_scale[None, :]).astype(jnp.bfloat16)


def shard_levels(key, dims, shards, least, high):
    def one(dim, blocks):
        steps = jax.random.uniform(jax.random.fold_in(jax.random.fold_in(key, 6), dim), (blocks,), jnp.float32, least / len(shards), high / len(shards))
        return jnp.repeat(jnp.exp(steps), dims[dim] // blocks).reshape((-1,) + (1,) * (len(dims) - dim - 1))

    gain = one(*shards[0])
    for cut in shards[1:]:
        gain = gain * one(*cut)
    return gain


def centred(rng, shape, spread, most, cuts=(), kind=jnp.bfloat16):
    level = shard_levels(rng, shape, cuts, -0.22, 0.18) if cuts else 1.0
    values = jax.random.normal(rng, shape, jnp.float32) * spread * level
    return jnp.minimum(jnp.maximum(values, -most), most).astype(kind)


def setup_inputs(seed: int = 0) -> dict:
    arg_keys = jax.random.split(jax.random.key(seed), 3)
    return {
        "bases": draw_bases(jax.random.fold_in(arg_keys[2], 71), 0),
        "start": centred(arg_keys[1], (COLS, M), 1.0, 6.0, ((0, 4),), jnp.float32),
    }


def reference(bases, start):
    row_blocks = bases.reshape(ROWS // ROWS_DEV, ROWS_DEV, COLS)

    def accumulate(carry, row_block):
        gram_matrix, energy = carry
        gram_matrix = gram_matrix + lax.dot_general(row_block.astype(jnp.float32), row_block.astype(jnp.float32), (((0,), (0,)), ((), ())), preferred_element_type=jnp.float32)
        energy = energy + jnp.sum(jnp.square(row_block.astype(jnp.float32)))
        return ((gram_matrix, energy), None)
    initial = (jnp.zeros((COLS, COLS), jnp.float32), jnp.zeros((), jnp.float32))
    (gram_matrix, energy), unused_out = lax.scan(accumulate, initial, row_blocks)
    diag_mean = energy / COLS
    q_now = start
    for iteration in range(ITERS):
        lifted = jnp.dot(gram_matrix, q_now, precision=lax.Precision.HIGHEST) / diag_mean + q_now
        correlation = lax.dot_general(lifted, lifted, (((0,), (0,)), ((), ())), precision=lax.Precision.HIGHEST)
        factor = jnp.linalg.cholesky(correlation)
        q_now = jax.scipy.linalg.solve_triangular(factor, lifted.T, lower=True).T
    q_low = q_now.astype(jnp.bfloat16)
    modes = jnp.dot(bases.astype(jnp.float32), q_low.astype(jnp.float32), preferred_element_type=jnp.float32)
    return modes.astype(jnp.bfloat16)
```

```python
import functools

import jax
import jax.numpy as jnp
from jax import lax
from jax.experimental import pallas as pl
from jax.experimental.pallas import tpu as pltpu
from jax.sharding import PartitionSpec as P

ITERS = 2
LANES = 128
SUB = 8
PANEL = 32
WIDE = 256
ORTHO_TOL = 2.0**-8
NN = ((1,), (0,))
TN = ((0,), (0,))
NT = ((1,), (1,))
f32 = jnp.float32
bf16 = jnp.bfloat16
VMEM = pl.BlockSpec(memory_space=pltpu.VMEM)
SMEM = pl.BlockSpec(memory_space=pltpu.SMEM)


def dot(left, right, dims):
    return lax.dot_general(left, right, (dims, ((), ())), preferred_element_type=f32)


def split(value):
    high = value.astype(bf16)
    return high, (value - high.astype(f32)).astype(bf16)


def dot_split(left, right, dims):
    return dot(left[0], right[0], dims) + dot(left[0], right[1], dims) + dot(left[1], right[0], dims)


def swap(value, axis, offset):
    size = lax.axis_size(axis)
    return lax.ppermute(value, axis, [(i, i ^ offset) for i in range(size)])


def pick(values, index):
    return lax.dynamic_index_in_dim(values, index, 0, keepdims=False)


def gram_blocks(parity, wide_ref, out_ref):
    chips, width, span = out_ref.shape
    for chip in range(chips):
        first = pl.multiple_of((2 * chip + parity) * width, width)
        out_ref[chip] = dot(wide_ref[:, pl.ds(first, width)], wide_ref[:, pl.ds(first, span)], TN)


def gram_send_kernel(at_ref, *refs):
    *pieces, wide_ref, out_ref = refs
    core, batch = at_ref[1], at_ref[2]
    basis = pieces[0].shape[1]
    columns = basis * len(pieces)
    for offset, piece in enumerate(pieces):
        first = pl.multiple_of(lax.bitwise_xor(batch, offset) * basis, basis)
        wide_ref[:, pl.ds(first, basis)] = piece[...]
    half = wide_ref.shape[1] - columns
    wide_ref[:, columns:] = wide_ref[:, :half]
    gram_blocks(1 - core, wide_ref, out_ref)


def gram_keep_kernel(at_ref, wide_ref, out_ref):
    gram_blocks(at_ref[1], wide_ref, out_ref)


def spread(value, index):
    return jnp.broadcast_to(value[index : index + 1, :], value.shape)


def factor_block(work):
    groups = PANEL // SUB
    sub = lax.broadcasted_iota(jnp.int32, (SUB, LANES), 0)
    for r0 in range(0, LANES, PANEL):
        m = [
            [work[r0 + SUB * g : r0 + SUB * (g + 1), LANES * t : LANES * (t + 1)] for t in range(2)]
            for g in range(groups)
        ]
        col = {}
        for j in range(PANEL):
            for g in range(j // SUB, groups):
                col[j, g] = jnp.broadcast_to(m[g][0][:, r0 + j : r0 + j + 1], (SUB, LANES))
        scale = [None] * groups
        for j in range(PANEL):
            gj, sj = divmod(j, SUB)
            pivot = spread(col[j, gj], sj)
            inverse = 1.0 / pivot
            root = lax.rsqrt(pivot)
            scale[gj] = root if scale[gj] is None else jnp.where(sub == sj, root, scale[gj])
            source = [spread(m[gj][t], sj) for t in range(2)]
            scaled = {g: col[j, g] * inverse for g in range(gj, groups)}
            for k in range(j + 1, PANEL):
                entry = spread(col[j, k // SUB], k % SUB)
                for g in range(k // SUB, groups):
                    col[k, g] = col[k, g] - scaled[g] * entry
            for g in range(gj, groups):
                factor = jnp.where(sub > sj, scaled[g], 0.0) if g == gj else scaled[g]
                for t in range(2):
                    m[g][t] = m[g][t] - factor * source[t]
        rows = jnp.concatenate(
            [jnp.concatenate([m[g][t] * scale[g] for t in range(2)], axis=1) for g in range(groups)], axis=0
        )
        work[r0 : r0 + PANEL, :] = rows
        below = r0 + PANEL
        if below < LANES:
            high, low = split(rows)
            left = jnp.concatenate([high[:, :LANES], high[:, :LANES], low[:, :LANES]], axis=0)
            right = jnp.concatenate([high, low, high], axis=0)
            work[below:, :] = work[below:, :] - dot(left, right, TN)[below:, :]


def identity(size):
    return lax.broadcasted_iota(jnp.int32, (size, size), 0) == lax.broadcasted_iota(jnp.int32, (size, size), 1)


def inverse_factor(a, e, x, work):
    size = a.shape[0]
    e[...] = identity(size).astype(f32)
    x[...] = jnp.zeros((size, size), f32)
    eye = identity(LANES).astype(f32)
    for lo in range(0, size, LANES):
        hi = lo + LANES
        work[:, :LANES] = a[lo:hi, lo:hi]
        work[:, LANES:] = eye
        factor_block(work)
        own = split(work[:, LANES:])
        x_rows = dot_split(own, split(e[lo:hi, :hi]), NN)
        x[lo:hi, :hi] = x_rows
        if hi < size:
            upper = split(dot_split(own, split(a[lo:hi, hi:]), NN))
            a[hi:, hi:] = a[hi:, hi:] - dot_split(upper, upper, TN)
            e[hi:, :hi] = e[hi:, :hi] - dot_split(upper, split(x_rows), TN)


def place_gram(at_ref, blocks, factor, high_ref, low_ref):
    chip, core, batch = at_ref[0], at_ref[1], at_ref[2]
    chips, parts, height, span = blocks[0].shape
    width = height * parts
    count = high_ref.shape[0] // width

    def place(offset, carry):
        for other, block in enumerate(blocks):
            i = 2 * lax.bitwise_xor(chip, offset) + lax.bitwise_xor(core, other)
            row = pl.multiple_of(i * width, width)
            for m in range(span // width):
                column = pl.multiple_of(lax.rem(i + m, count) * width, width)
                for part in range(parts):
                    inner = pl.multiple_of(row + lax.bitwise_xor(batch, part) * height, height)
                    high, low = split(block[offset, part, :, m * width : (m + 1) * width] * factor)
                    high_ref[pl.ds(inner, height), pl.ds(column, width)] = high
                    low_ref[pl.ds(inner, height), pl.ds(column, width)] = low
                if 0 < 2 * m < count:
                    for ref in (high_ref, low_ref):
                        tile = ref[pl.ds(row, width), pl.ds(column, width)]
                        ref[pl.ds(column, width), pl.ds(row, width)] = tile.T
        return carry

    lax.fori_loop(0, chips, place, 0)


def gram_trace(at_ref, blocks):
    batch = at_ref[2]
    chips, parts, height, span = blocks[0].shape
    width = height * parts
    rows = lax.broadcasted_iota(jnp.int32, (height, width), 0)
    lanes = lax.broadcasted_iota(jnp.int32, (height, width), 1)

    def add(offset, total):
        for block in blocks:
            for part in range(parts):
                on = lanes == rows + lax.bitwise_xor(batch, part) * height
                total = total + jnp.where(on, block[offset, part, :, :width], 0.0)
        return total

    return jnp.sum(lax.fori_loop(0, chips, add, jnp.zeros((height, width), f32)))


def solve_kernel(at_ref, own, sibling, start, rows, modes, error, ah, al, ph, plo, qh, ql, a, e, x, work):
    size, columns = start.shape
    blocks = (own, sibling)
    factor = 1.0 / (gram_trace(at_ref, blocks) / columns)
    place_gram(at_ref, blocks, factor, ah, al)
    ph[...], plo[...] = split(start[...])

    def lift(source, target):
        def chunk(n, carry):
            at = pl.ds(pl.multiple_of(n * WIDE, WIDE), WIDE)
            before = source[0][:, at].astype(f32) + source[1][:, at].astype(f32)
            after = before + dot_split((source[0][...], source[1][...]), (ah[:, at], al[:, at]), NN)
            target[0][:, at], target[1][:, at] = split(after)
            return carry

        lax.fori_loop(0, columns // WIDE, chunk, 0)

    lift((ph, plo), (qh, ql))
    lift((qh, ql), (ph, plo))
    for lo in range(0, size, LANES):
        hi = lo + LANES
        a[lo:hi, lo:] = dot_split((ph[lo:hi], plo[lo:hi]), (ph[lo:], plo[lo:]), NT)
    inverse_factor(a, e, x, work)
    for lo in range(0, size, LANES):
        hi = lo + LANES
        qh[lo:hi] = dot_split(split(x[lo:hi, :hi]), (ph[:hi], plo[:hi]), NN).astype(bf16)
    worst = jnp.zeros((), f32)
    for lo in range(0, size, LANES):
        gap = dot(qh[lo : lo + LANES], qh[...], NT)
        here = lax.broadcasted_iota(jnp.int32, gap.shape, 0) + lo == lax.broadcasted_iota(jnp.int32, gap.shape, 1)
        gap = gap - here.astype(f32)
        worst = jnp.maximum(worst, jnp.max(jnp.sum(gap * gap, axis=1, keepdims=True)))
    error[0] = worst
    for lo in range(0, size, WIDE):
        modes[:, lo : lo + WIDE] = dot(rows[...], qh[lo : lo + WIDE], NT).astype(bf16)


def place_kernel(at_ref, own, sibling, gram):
    chip, core, batch = at_ref[0], at_ref[1], at_ref[2]
    chips, parts, height, span = own.shape
    width = height * parts
    count = gram.shape[0] // width

    def place(offset, carry):
        for other, block in enumerate((own, sibling)):
            i = 2 * lax.bitwise_xor(chip, offset) + lax.bitwise_xor(core, other)
            row = pl.multiple_of(i * width, width)
            for m in range(span // width):
                column = pl.multiple_of(lax.rem(i + m, count) * width, width)
                for part in range(parts):
                    inner = pl.multiple_of(row + lax.bitwise_xor(batch, part) * height, height)
                    gram[pl.ds(inner, height), pl.ds(column, width)] = block[
                        offset, part, :, m * width : (m + 1) * width
                    ]
                if 0 < 2 * m < count:
                    gram[pl.ds(column, width), pl.ds(row, width)] = gram[pl.ds(row, width), pl.ds(column, width)].T
        return carry

    lax.fori_loop(0, chips, place, 0)


def step_by_step(at, own, sibling, start_rows, rows):
    columns = start_rows.shape[1]
    gram = pl.pallas_call(
        place_kernel,
        out_shape=jax.ShapeDtypeStruct((columns, columns), f32),
        in_specs=[SMEM, VMEM, VMEM],
        out_specs=VMEM,
        compiler_params=pltpu.CompilerParams(vmem_limit_bytes=48 << 20),
    )(at, own, sibling)
    diag_mean = jnp.trace(gram) / columns
    q = start_rows.T
    for _ in range(ITERS):
        lifted = jnp.dot(gram, q, precision=lax.Precision.HIGHEST) / diag_mean + q
        correlation = lax.dot_general(lifted, lifted, (TN, ((), ())), precision=lax.Precision.HIGHEST)
        factor = jnp.linalg.cholesky(correlation)
        q = jax.scipy.linalg.solve_triangular(factor, lifted.T, lower=True).T
    return dot(rows, q.astype(bf16), NN).astype(bf16)


def on_device(bases, start):
    local_rows, basis = bases.shape
    size = start.shape[1]
    n_batch, n_rows = lax.axis_size("batch"), lax.axis_size("rows")
    chips = n_rows // 2
    columns = basis * n_batch
    sub_rows = local_rows // n_batch
    width = columns // n_rows
    span = width * (chips + 1)
    height = width // n_batch
    batch, row = lax.axis_index("batch"), lax.axis_index("rows")
    chip, core = row // 2, row % 2
    at = jnp.stack([chip, core, batch]).astype(jnp.int32)
    params = pltpu.CompilerParams(vmem_limit_bytes=60 << 20)

    pieces = []
    for offset in range(n_batch):
        piece = lax.dynamic_slice_in_dim(bases, (batch ^ offset) * sub_rows, sub_rows, 0)
        pieces.append(swap(piece, "batch", offset) if offset else piece)

    share = start.shape[0] // n_rows
    start_share = lax.dynamic_slice_in_dim(start, row * share, share, 0)
    start_rows = lax.all_gather(start_share, ("batch", "rows"), axis=0, tiled=True).T

    wide, send = pl.pallas_call(
        gram_send_kernel,
        out_shape=(
            jax.ShapeDtypeStruct((sub_rows, columns + columns // 2), bf16),
            jax.ShapeDtypeStruct((chips, width, span), f32),
        ),
        in_specs=[SMEM] + [VMEM] * n_batch,
        out_specs=(VMEM, VMEM),
        compiler_params=params,
        cost_estimate=pl.CostEstimate(flops=sub_rows * span * columns, bytes_accessed=5 << 20, transcendentals=0),
    )(at, *pieces)
    keep = pl.pallas_call(
        gram_keep_kernel,
        out_shape=jax.ShapeDtypeStruct((chips, width, span), f32),
        in_specs=[SMEM, VMEM],
        out_specs=VMEM,
        compiler_params=params,
        cost_estimate=pl.CostEstimate(flops=sub_rows * span * columns, bytes_accessed=4 << 20, transcendentals=0),
    )(at, wide)

    total = keep + swap(send, "rows", 1)
    block = pick(total, chip)
    for offset in range(1, chips):
        block = block + swap(pick(total, chip ^ offset), "rows", 2 * offset)
    parts = block.reshape(n_batch, height, span)
    part = pick(parts, batch)
    for offset in range(1, n_batch):
        part = part + swap(pick(parts, batch ^ offset), "batch", offset)

    block = jnp.stack([part] + [swap(part, "batch", offset) for offset in range(1, n_batch)])
    own = jnp.stack([block] + [swap(block, "rows", 2 * offset) for offset in range(1, chips)])
    sibling = swap(own, "rows", 1)

    wide_rows = wide[:, :columns]
    modes, error = pl.pallas_call(
        solve_kernel,
        out_shape=(jax.ShapeDtypeStruct((sub_rows, size), bf16), jax.ShapeDtypeStruct((1,), f32)),
        in_specs=[SMEM] + [VMEM] * 4,
        out_specs=(VMEM, SMEM),
        scratch_shapes=[pltpu.VMEM((columns, columns), bf16)] * 2
        + [pltpu.VMEM((size, columns), bf16)] * 4
        + [pltpu.VMEM((size, size), f32)] * 3
        + [pltpu.VMEM((LANES, 2 * LANES), f32)],
        compiler_params=params,
    )(at, own, sibling, start_rows, wide_rows)
    return lax.cond(
        error[0] < ORTHO_TOL**2,
        lambda *_: modes,
        step_by_step,
        at, own, sibling, start_rows, wide_rows,
    )


def solution(mesh):
    in_specs = (P("rows", "batch"), P("batch", None))
    out_specs = P(("rows", "batch"), None)
    return jax.shard_map(
        on_device, mesh=mesh, in_specs=in_specs, out_specs=out_specs, check_vma=False
    )
```

```python
import functools

import jax
import jax.numpy as jnp
from jax import lax
from jax.experimental import pallas as pl
from jax.experimental.pallas import tpu as pltpu
from jax.sharding import PartitionSpec as P

ITERS = 2
LANES = 128
SUB = 8
PANEL = 32
REPEAT = 4
SHIFT = 2.0**-15
WIDE = 256
ORTHO_TOL = 2.0**-8
NN = ((1,), (0,))
TN = ((0,), (0,))
NT = ((1,), (1,))
f32 = jnp.float32
bf16 = jnp.bfloat16
VMEM = pl.BlockSpec(memory_space=pltpu.VMEM)
SMEM = pl.BlockSpec(memory_space=pltpu.SMEM)


def dot(left, right, dims):
    return lax.dot_general(left, right, (dims, ((), ())), preferred_element_type=f32)


def split(value):
    high = value.astype(bf16)
    return high, (value - high.astype(f32)).astype(bf16)


def dot_split(left, right, dims):
    return dot(left[0], right[0], dims) + dot(left[0], right[1], dims) + dot(left[1], right[0], dims)


def swap(value, axis, offset):
    size = lax.axis_size(axis)
    return lax.ppermute(value, axis, [(i, i ^ offset) for i in range(size)])


def spans(count, size):
    return [slice(i * size, (i + 1) * size) for i in range(count)]


def tile_table(n_batch, per_basis, n_rows):
    tiles = [
        (first * per_basis + i, second * per_basis + j)
        for first in range(n_batch)
        for second in range(first + 1, n_batch)
        for i in range(per_basis)
        for j in range(per_basis)
    ]
    share = -(-len(tiles) // n_rows)
    return tiles + tiles[-1:] * (share * n_rows - len(tiles)), share


def own_tiles(per_basis):
    return [(i, j) for i in range(per_basis) for j in range(i, per_basis)]


def spread_copy(value, axis, offsets):
    return jnp.stack([value] + [swap(value, axis, offset) for offset in offsets])


def diagonal_kernel(bases, out):
    per_basis = bases.shape[1] // LANES
    columns = spans(per_basis, LANES)
    for at, (i, j) in zip(spans(len(own_tiles(per_basis)), LANES), own_tiles(per_basis)):
        out[at] = dot(bases[:, columns[i]], bases[:, columns[j]], TN)


def cross_kernel(at_ref, table, *refs):
    chips = lax.axis_size("rows") // 2
    n_batch = lax.axis_size("batch")
    pieces, (rows, *outs, both) = refs[: 2 * n_batch], refs[2 * n_batch :]
    chip, core, batch = at_ref[0], at_ref[1], at_ref[2]
    sub_rows, basis = pieces[0].shape
    for half in range(2):
        for offset in range(n_batch):
            first = pl.multiple_of(lax.bitwise_xor(batch, offset) * basis, basis)
            both[half * sub_rows : (half + 1) * sub_rows, pl.ds(first, basis)] = pieces[half * n_batch + offset][...]
    rows[...] = both[:sub_rows]
    for offset, out in enumerate(outs):
        share = out.shape[0] // LANES
        owner = 2 * lax.bitwise_xor(chip, offset) + core
        for j, at in enumerate(spans(share, LANES)):
            place = 2 * (owner * share + j)
            left = pl.multiple_of(table[place] * LANES, LANES)
            right = pl.multiple_of(table[place + 1] * LANES, LANES)
            out[at] = dot(both[:, pl.ds(left, LANES)], both[:, pl.ds(right, LANES)], TN)


def share_kernel(at_ref, *refs):
    n_batch = lax.axis_size("batch")
    blocks, outs = refs[:-n_batch], refs[-n_batch:]
    batch = at_ref[2]
    height = LANES // n_batch
    for offset, out in enumerate(outs):
        first = pl.multiple_of(lax.bitwise_xor(batch, offset) * height, height)
        for j, at in enumerate(spans(out.shape[0] // height, height)):
            rows = pl.ds(j * LANES + first, height)
            total = blocks[0][rows, :]
            for block in blocks[1:]:
                total = total + block[rows, :]
            out[at] = total


def spread(value, index):
    return jnp.broadcast_to(value[index : index + 1, :], value.shape)


def factor_block(work):
    groups = PANEL // SUB
    sub = lax.broadcasted_iota(jnp.int32, (SUB, LANES), 0)
    for r0 in range(0, LANES, PANEL):
        m = [
            [work[r0 + SUB * g : r0 + SUB * (g + 1), LANES * t : LANES * (t + 1)] for t in range(2)]
            for g in range(groups)
        ]
        col = {}
        for j in range(PANEL):
            for g in range(j // SUB, groups):
                col[j, g] = jnp.broadcast_to(m[g][0][:, r0 + j : r0 + j + 1], (SUB, LANES))
        scale = [None] * groups
        for j in range(PANEL):
            gj, sj = divmod(j, SUB)
            pivot = spread(col[j, gj], sj)
            inverse = 1.0 / pivot
            root = lax.rsqrt(pivot)
            scale[gj] = root if scale[gj] is None else jnp.where(sub == sj, root, scale[gj])
            source = [spread(m[gj][t], sj) for t in range(2)]
            scaled = {g: col[j, g] * inverse for g in range(gj, groups)}
            for k in range(j + 1, PANEL):
                entry = spread(col[j, k // SUB], k % SUB)
                for g in range(k // SUB, groups):
                    col[k, g] = col[k, g] - scaled[g] * entry
            for g in range(gj, groups):
                factor = jnp.where(sub > sj, scaled[g], 0.0) if g == gj else scaled[g]
                for t in range(2):
                    m[g][t] = m[g][t] - factor * source[t]
        rows = jnp.concatenate(
            [jnp.concatenate([m[g][t] * scale[g] for t in range(2)], axis=1) for g in range(groups)], axis=0
        )
        work[r0 : r0 + PANEL, :] = rows
        below = r0 + PANEL
        if below < LANES:
            high, low = split(rows)
            left = jnp.concatenate([high[:, :LANES], high[:, :LANES], low[:, :LANES]], axis=0)
            right = jnp.concatenate([high, low, high], axis=0)
            work[below:, :] = work[below:, :] - dot(left, right, TN)[below:, :]


def identity(size):
    return lax.broadcasted_iota(jnp.int32, (size, size), 0) == lax.broadcasted_iota(jnp.int32, (size, size), 1)


def inverse_factor(a, e, x, work):
    size = a.shape[0]
    e[...] = identity(size).astype(f32)
    lanes = lax.broadcasted_iota(jnp.int32, (LANES, size), 1)

    def block(k, carry):
        at = pl.ds(pl.multiple_of(k * LANES, LANES), LANES)
        work[:, :LANES] = a[at, at]
        work[:, LANES:] = identity(LANES).astype(f32)
        factor_block(work)
        own = split(work[:, LANES:])
        x_rows = dot_split(own, split(e[at, :]), NN)
        x[at, :] = x_rows
        upper = dot_split(own, split(a[at, :]), NN)
        upper = split(jnp.where(lanes >= (k + 1) * LANES, upper, 0.0))
        a[...] = a[...] - dot_split(upper, upper, TN)
        e[...] = e[...] - dot_split(upper, split(x_rows), TN)
        return carry

    lax.fori_loop(0, size // LANES, block, 0)


def prepare_kernel(at_ref, own, sibling, high, low, diagonal, whole):
    chip, core, batch = at_ref[0], at_ref[1], at_ref[2]
    chips, n_batch, height, _ = own.shape
    columns, size = whole.shape
    basis = columns // n_batch
    share = basis // (2 * chips)
    part = diagonal.shape[1] // (2 * chips)

    def place(offset, carry):
        for other, block in enumerate((own, sibling)):
            row = 2 * lax.bitwise_xor(chip, offset) + lax.bitwise_xor(core, other)
            for z in range(n_batch):
                group = lax.bitwise_xor(batch, z)
                diagonal[group, pl.ds(pl.multiple_of(row * part, SUB), part), :] = block[offset, z, :part, :]
                first = pl.multiple_of(group * basis + row * share, SUB)
                for k, lanes in enumerate(spans(size // LANES, LANES)):
                    lower = part + k * share
                    whole[pl.ds(first, share), lanes] = block[offset, z, lower : lower + share, :]
        return carry

    lax.fori_loop(0, chips, place, 0)
    for rows in spans(columns // LANES, LANES):
        high[:, rows], low[:, rows] = split(whole[rows, :].T)


def trace_of(diagonal, per_basis):
    total = jnp.zeros((LANES, LANES), f32)
    eye = identity(LANES)
    for group in range(diagonal.shape[0]):
        for at, (i, j) in zip(spans(len(own_tiles(per_basis)), LANES), own_tiles(per_basis)):
            if i == j:
                total = total + jnp.where(eye, diagonal[group, at, :], 0.0)
    return jnp.sum(total)


def place_gram(at_ref, table, own, sibling, diagonal, factor, pair):
    chip, core, batch = at_ref[0], at_ref[1], at_ref[2]
    chips, n_batch, share_rows, _ = own.shape
    height = LANES // n_batch
    share = share_rows // height
    per_basis = pair[0].shape[0] // LANES // n_batch

    def place(offset, carry):
        for other, block in enumerate((own, sibling)):
            owner = 2 * lax.bitwise_xor(chip, offset) + lax.bitwise_xor(core, other)
            for j, inner in enumerate(spans(share, height)):
                at = 2 * (owner * share + j)
                row = pl.multiple_of(table[at] * LANES, LANES)
                column = pl.multiple_of(table[at + 1] * LANES, LANES)
                for z in range(n_batch):
                    first = pl.multiple_of(row + lax.bitwise_xor(batch, z) * height, height)
                    for ref, value in zip(pair, split(block[offset, z, inner, :] * factor)):
                        ref[pl.ds(first, height), pl.ds(column, LANES)] = value
                for ref in pair:
                    ref[pl.ds(column, LANES), pl.ds(row, LANES)] = ref[pl.ds(row, LANES), pl.ds(column, LANES)].T
        return carry

    lax.fori_loop(0, chips, place, 0)
    for group in range(n_batch):
        for at, (i, j) in zip(spans(len(own_tiles(per_basis)), LANES), own_tiles(per_basis)):
            rows, columns = (slice((group * per_basis + k) * LANES, (group * per_basis + k + 1) * LANES) for k in (i, j))
            for ref, value in zip(pair, split(diagonal[group, at, :] * factor)):
                ref[rows, columns] = value
                if i != j:
                    ref[columns, rows] = value.T


def solve_kernel(at_ref, table, own, sibling, diagonal, sh, sl, rows, modes, ah, al, ph, plo, qh, ql, a, e, x, work):
    size, columns = sh.shape
    per_basis = columns // LANES // own.shape[1]
    gram, p, q = (ah, al), (ph, plo), (qh, ql)
    factor = 1.0 / (trace_of(diagonal, per_basis) / columns)
    place_gram(at_ref, table, own, sibling, diagonal, factor, gram)

    def lift(source, target):
        def chunk(n, carry):
            at = pl.ds(pl.multiple_of(n * WIDE, WIDE), WIDE)
            before = source[0][:, at].astype(f32) + source[1][:, at].astype(f32)
            after = before + dot_split((source[0][...], source[1][...]), (gram[0][:, at], gram[1][:, at]), NN)
            target[0][:, at], target[1][:, at] = split(after)
            return carry

        lax.fori_loop(0, columns // WIDE, chunk, 0)

    def correlate():
        for at in spans(size // LANES, LANES):
            a[at, at.start :] = dot_split((ph[at], plo[at]), (ph[at.start :], plo[at.start :]), NT)

    def rotate():
        for at in spans(size // LANES, LANES):
            turned = dot_split(split(x[at, : at.stop]), (ph[: at.stop], plo[: at.stop]), NN)
            qh[at], ql[at] = split(turned)

    lift((sh, sl), q)
    lift(q, p)
    correlate()
    inverse_factor(a, e, x, work)
    rotate()

    worst = jnp.zeros((), f32)
    for at in spans(size // LANES, LANES):
        gap = dot(qh[at], qh[...], NT)
        here = lax.broadcasted_iota(jnp.int32, gap.shape, 0) + at.start == lax.broadcasted_iota(jnp.int32, gap.shape, 1)
        gap = gap - here.astype(f32)
        worst = jnp.maximum(worst, jnp.max(jnp.sum(gap * gap, axis=1, keepdims=True)))

    @pl.when(jnp.logical_not(worst < ORTHO_TOL**2))
    def _():
        qh[...], ql[...] = sh[...], sl[...]

        def again(k, carry):
            turn = lax.rem(k, REPEAT)

            @pl.when(turn == 0)
            def _():
                lift(q, p)

            @pl.when(turn != 0)
            def _():
                ph[...], plo[...] = qh[...], ql[...]

            correlate()

            @pl.when(turn < 2)
            def _():
                eye = identity(LANES)
                tiles = [a[at, at] for at in spans(size // LANES, LANES)]
                shift = SHIFT * jnp.sum(sum(jnp.where(eye, tile, 0.0) for tile in tiles))
                for at, tile in zip(spans(size // LANES, LANES), tiles):
                    a[at, at] = tile + jnp.where(eye, shift, 0.0)

            inverse_factor(a, e, x, work)
            rotate()
            return carry

        lax.fori_loop(0, ITERS * REPEAT, again, 0)

    for lo in range(0, size, WIDE):
        modes[:, lo : lo + WIDE] = dot(rows[...], qh[lo : lo + WIDE], NT).astype(bf16)


def on_device(bases, start):
    local_rows, basis = bases.shape
    size = start.shape[1]
    n_batch, n_rows = lax.axis_size("batch"), lax.axis_size("rows")
    chips = n_rows // 2
    columns = basis * n_batch
    sub_rows = local_rows // n_batch
    per_basis = basis // LANES
    batch, row = lax.axis_index("batch"), lax.axis_index("rows")
    at = jnp.stack([row // 2, row % 2, batch]).astype(jnp.int32)
    tiles, share = tile_table(n_batch, per_basis, n_rows)
    table = jnp.asarray([k for tile in tiles for k in tile], jnp.int32)
    other_batches, other_chips = range(1, n_batch), range(2, n_rows, 2)

    def call(kernel, outs, scratch, *args, n_smem=0, flops=0, moved=1 << 20):
        return pl.pallas_call(
            kernel,
            out_shape=[jax.ShapeDtypeStruct(shape, dtype) for shape, dtype in outs],
            in_specs=[SMEM] * n_smem + [VMEM] * (len(args) - n_smem),
            out_specs=[VMEM] * len(outs),
            scratch_shapes=[pltpu.VMEM(shape, dtype) for shape, dtype in scratch],
            compiler_params=pltpu.CompilerParams(vmem_limit_bytes=60 << 20),
            cost_estimate=pl.CostEstimate(flops=flops, bytes_accessed=moved, transcendentals=0),
        )(*args)

    pieces = []
    for offset in range(n_batch):
        piece = lax.dynamic_slice_in_dim(bases, (batch ^ offset) * sub_rows, sub_rows, 0)
        pieces.append(swap(piece, "batch", offset) if offset else piece)
    other_pieces = [swap(piece, "rows", 1) for piece in pieces]

    own_count = len(own_tiles(per_basis))
    (diagonal,) = call(
        diagonal_kernel, [((own_count * LANES, LANES), f32)], [], bases,
        flops=2 * local_rows * own_count * LANES * LANES, moved=bases.size * 2,
    )
    for offset in (1 << k for k in range(n_rows.bit_length() - 1)):
        diagonal = diagonal + swap(diagonal, "rows", offset)
    part = own_count * LANES // n_rows
    start_share = start.shape[0] // n_rows
    mine = lax.dynamic_slice_in_dim(start, row * start_share, start_share, 0)
    mine = [lax.dynamic_slice_in_dim(diagonal, row * part, part, 0)] + jnp.split(mine, size // LANES, axis=1)
    mine = spread_copy(jnp.concatenate(mine), "batch", other_batches)
    mine = spread_copy(mine, "rows", other_chips)
    high, low, diagonal = call(
        prepare_kernel,
        [((size, columns), bf16)] * 2 + [((n_batch, own_count * LANES, LANES), f32)],
        [((columns, size), f32)],
        at, mine, swap(mine, "rows", 1), n_smem=1, moved=8 << 20,
    )

    rows, *blocks = call(
        cross_kernel,
        [((sub_rows, columns), bf16)] + [((share * LANES, LANES), f32)] * chips,
        [((2 * sub_rows, columns), bf16)],
        at, table, *pieces, *other_pieces, n_smem=2,
        flops=4 * sub_rows * chips * share * LANES * LANES, moved=6 << 20,
    )
    blocks = [blocks[0]] + [swap(block, "rows", offset) for block, offset in zip(blocks[1:], other_chips)]
    height = LANES // n_batch
    parts = call(share_kernel, [((share * height, LANES), f32)] * n_batch, [], at, *blocks, n_smem=1)
    total = sum((swap(parts[offset], "batch", offset) for offset in other_batches), parts[0])

    own = spread_copy(spread_copy(total, "batch", other_batches), "rows", other_chips)
    (modes,) = call(
        solve_kernel,
        [((sub_rows, size), bf16)],
        [((columns, columns), bf16)] * 2
        + [((size, columns), bf16)] * 4
        + [((size, size), f32)] * 3
        + [((LANES, 2 * LANES), f32)],
        at, table, own, swap(own, "rows", 1), diagonal, high, low, rows, n_smem=2, flops=10**10, moved=10 << 20,
    )
    return modes


def solution(mesh):
    in_specs = (P("rows", "batch"), P("batch", None))
    out_specs = P(("rows", "batch"), None)
    return jax.shard_map(
        on_device, mesh=mesh, in_specs=in_specs, out_specs=out_specs, check_vma=False
    )
```

```python
import functools

import jax
import jax.numpy as jnp
from jax import lax
from jax.experimental import pallas as pl
from jax.experimental.pallas import tpu as pltpu
from jax.sharding import PartitionSpec as P

ITERS = 2
LANES = 128
SUB = 8
PANEL = 32
REPEAT = 4
SHIFT = 2.0**-15
WIDE = 256
ORTHO_TOL = 2.0**-8
NN = ((1,), (0,))
TN = ((0,), (0,))
NT = ((1,), (1,))
f32 = jnp.float32
bf16 = jnp.bfloat16
f16 = jnp.float16
SCALE = 32.0
VMEM = pl.BlockSpec(memory_space=pltpu.VMEM)
ANY = pl.BlockSpec(memory_space=pl.ANY)
SMEM = pl.BlockSpec(memory_space=pltpu.SMEM)


def dot(left, right, dims):
    return lax.dot_general(left, right, (dims, ((), ())), preferred_element_type=f32)


def split(value):
    high = value.astype(bf16)
    return high, (value - high.astype(f32)).astype(bf16)


def dot_split(left, right, dims):
    return dot(left[0], right[0], dims) + dot(left[0], right[1], dims) + dot(left[1], right[0], dims)


def swap(value, axis, offset):
    size = lax.axis_size(axis)
    return lax.ppermute(value, axis, [(i, i ^ offset) for i in range(size)])


def spans(count, size):
    return [slice(i * size, (i + 1) * size) for i in range(count)]


def tile_table(n_batch, per_basis, n_rows):
    tiles = [
        (first * per_basis + i, second * per_basis + j)
        for first in range(n_batch)
        for second in range(first + 1, n_batch)
        for i in range(per_basis)
        for j in range(per_basis)
    ]
    share = -(-len(tiles) // n_rows)
    return tiles + tiles[-1:] * (share * n_rows - len(tiles)), share


def own_tiles(per_basis):
    return [(i, j) for i in range(per_basis) for j in range(i, per_basis)]


def spread_copy(value, axis, offsets):
    return jnp.stack([value] + [swap(value, axis, offset) for offset in offsets])


def diagonal_kernel(bases, out):
    per_basis = bases.shape[1] // LANES
    columns = spans(per_basis, LANES)
    energy = jnp.zeros((SUB, LANES), f32)
    for at, (i, j) in zip(spans(len(own_tiles(per_basis)), LANES), own_tiles(per_basis)):
        tile = dot(bases[:, columns[i]], bases[:, columns[j]], TN)
        out[at] = tile
        if i == j:
            tile = jnp.where(identity(LANES), tile, 0.0)
            energy = energy + sum(tile[rows] for rows in spans(LANES // SUB, SUB))
    out[at.stop :] = energy


def cross_kernel(at_ref, table, scale, start, diagonal, *refs):
    n_batch = lax.axis_size("batch")
    pieces, (rows, message, *outs, both) = refs[: 2 * n_batch], refs[2 * n_batch :]
    chip, core, batch = at_ref[0], at_ref[1], at_ref[2]
    sub_rows, basis = pieces[0].shape
    for half in range(2):
        for offset in range(n_batch):
            first = pl.multiple_of(lax.bitwise_xor(batch, offset) * basis, basis)
            both[half * sub_rows : (half + 1) * sub_rows, pl.ds(first, basis)] = pieces[half * n_batch + offset][...]
    rows[...] = both[:sub_rows]
    index = 2 * chip + core
    share, size = start.shape[0] // lax.axis_size("rows"), start.shape[1]
    part = message.shape[0] - share * size // LANES
    message[:part] = diagonal[pl.ds(pl.multiple_of(index * part, SUB), part), :]
    for k, lanes in enumerate(spans(size // LANES, LANES)):
        first = pl.multiple_of(index * share, SUB)
        message[part + k * share : part + (k + 1) * share] = start[pl.ds(first, share), lanes]
    for offset, out in enumerate(outs):
        share = out.shape[0] // LANES
        owner = 2 * lax.bitwise_xor(chip, offset) + core
        for j, at in enumerate(spans(share, LANES)):
            place = 2 * (owner * share + j)
            left = pl.multiple_of(table[place] * LANES, LANES)
            right = pl.multiple_of(table[place + 1] * LANES, LANES)
            out[at] = dot(both[:, pl.ds(left, LANES)], both[:, pl.ds(right, LANES)], TN) * scale[0]


def spread(value, index):
    return jnp.broadcast_to(value[index : index + 1, :], value.shape)


def factor_block(work):
    groups = PANEL // SUB
    sub = lax.broadcasted_iota(jnp.int32, (SUB, LANES), 0)
    for r0 in range(0, LANES, PANEL):
        m = [
            [work[r0 + SUB * g : r0 + SUB * (g + 1), LANES * t : LANES * (t + 1)] for t in range(2)]
            for g in range(groups)
        ]
        col = {}
        for j in range(PANEL):
            for g in range(j // SUB, groups):
                col[j, g] = jnp.broadcast_to(m[g][0][:, r0 + j : r0 + j + 1], (SUB, LANES))
        scale = [None] * groups
        for j in range(PANEL):
            gj, sj = divmod(j, SUB)
            pivot = spread(col[j, gj], sj)
            inverse = 1.0 / pivot
            root = lax.rsqrt(pivot)
            scale[gj] = root if scale[gj] is None else jnp.where(sub == sj, root, scale[gj])
            source = [spread(m[gj][t], sj) for t in range(2)]
            scaled = {g: col[j, g] * inverse for g in range(gj, groups)}
            for k in range(j + 1, PANEL):
                entry = spread(col[j, k // SUB], k % SUB)
                for g in range(k // SUB, groups):
                    col[k, g] = col[k, g] - scaled[g] * entry
            for g in range(gj, groups):
                factor = jnp.where(sub > sj, scaled[g], 0.0) if g == gj else scaled[g]
                for t in range(2):
                    m[g][t] = m[g][t] - factor * source[t]
        rows = jnp.concatenate(
            [jnp.concatenate([m[g][t] * scale[g] for t in range(2)], axis=1) for g in range(groups)], axis=0
        )
        work[r0 : r0 + PANEL, :] = rows
        below = r0 + PANEL
        if below < LANES:
            high, low = split(rows)
            left = jnp.concatenate([high[:, :LANES], high[:, :LANES], low[:, :LANES]], axis=0)
            right = jnp.concatenate([high, low, high], axis=0)
            work[below:, :] = work[below:, :] - dot(left, right, TN)[below:, :]


def identity(size):
    return lax.broadcasted_iota(jnp.int32, (size, size), 0) == lax.broadcasted_iota(jnp.int32, (size, size), 1)


def inverse_factor(a, e, x, work):
    size = a.shape[0]
    e[...] = identity(size).astype(f32)
    lanes = lax.broadcasted_iota(jnp.int32, (LANES, size), 1)

    def block(k, carry):
        at = pl.ds(pl.multiple_of(k * LANES, LANES), LANES)
        work[:, :LANES] = a[at, at]
        work[:, LANES:] = identity(LANES).astype(f32)
        factor_block(work)
        own = split(work[:, LANES:])
        x_rows = dot_split(own, split(e[at, :]), NN)
        x[at, :] = x_rows
        upper = dot_split(own, split(a[at, :]), NN)
        upper = split(jnp.where(lanes >= (k + 1) * LANES, upper, 0.0))
        a[...] = a[...] - dot_split(upper, upper, TN)
        e[...] = e[...] - dot_split(upper, split(x_rows), TN)
        return carry

    lax.fori_loop(0, size // LANES, block, 0)


def prepare_kernel(at_ref, *refs):
    *blocks, high, low, diagonal, whole = refs
    chip, core, batch = at_ref[0], at_ref[1], at_ref[2]
    n_batch = blocks[0].shape[0]
    columns, size = whole.shape
    basis = columns // n_batch
    share = basis // len(blocks)
    part = diagonal.shape[1] // len(blocks)
    for k, block in enumerate(blocks):
        other, offset = divmod(k, len(blocks) // 2)
        row = 2 * lax.bitwise_xor(chip, offset) + lax.bitwise_xor(core, other)
        for z in range(n_batch):
            group = lax.bitwise_xor(batch, z)
            diagonal[group, pl.ds(pl.multiple_of(row * part, SUB), part), :] = block[z, :part, :]
            first = pl.multiple_of(group * basis + row * share, SUB)
            for k, lanes in enumerate(spans(size // LANES, LANES)):
                lower = part + k * share
                whole[pl.ds(first, share), lanes] = block[z, lower : lower + share, :]
    for rows in spans(columns // LANES, LANES):
        high[:, rows], low[:, rows] = split(whole[rows, :].T)


def trace_of(diagonal, per_basis):
    total = jnp.zeros((LANES, LANES), f32)
    eye = identity(LANES)
    for group in range(diagonal.shape[0]):
        for at, (i, j) in zip(spans(len(own_tiles(per_basis)), LANES), own_tiles(per_basis)):
            if i == j:
                total = total + jnp.where(eye, diagonal[group, at, :], 0.0)
    return jnp.sum(total)


def place_gram(at_ref, table, cross, diagonal, factor, pair):
    chip, core = at_ref[0], at_ref[1]
    devices, share_rows, _ = cross.shape
    share = share_rows // LANES
    n_batch = diagonal.shape[0]
    per_basis = pair[0].shape[0] // LANES // n_batch

    def place(k, carry):
        other, offset = k // (devices // 2), lax.rem(k, devices // 2)
        owner = 2 * lax.bitwise_xor(chip, offset) + lax.bitwise_xor(core, other)
        for j, inner in enumerate(spans(share, LANES)):
            at = 2 * (owner * share + j)
            row = pl.ds(pl.multiple_of(table[at] * LANES, LANES), LANES)
            column = pl.ds(pl.multiple_of(table[at + 1] * LANES, LANES), LANES)
            for ref, value in zip(pair, split(cross[k, inner, :] * (1.0 / SCALE))):
                ref[row, column] = value
                ref[column, row] = value.T
        return carry

    lax.fori_loop(0, devices, place, 0)
    for group in range(n_batch):
        for at, (i, j) in zip(spans(len(own_tiles(per_basis)), LANES), own_tiles(per_basis)):
            rows, columns = (slice((group * per_basis + k) * LANES, (group * per_basis + k + 1) * LANES) for k in (i, j))
            for ref, value in zip(pair, split(diagonal[group, at, :] * factor)):
                ref[rows, columns] = value
                if i != j:
                    ref[columns, rows] = value.T


def solve_kernel(at_ref, table, cross, diagonal, sh, sl, rows, modes, ah, al, ph, plo, qh, ql, a, e, x, work):
    size, columns = sh.shape
    per_basis = columns // LANES // diagonal.shape[0]
    gram, p, q = (ah, al), (ph, plo), (qh, ql)
    factor = 1.0 / (trace_of(diagonal, per_basis) / columns)
    place_gram(at_ref, table, cross, diagonal, factor, gram)

    def lift(source, target):
        def chunk(n, carry):
            at = pl.ds(pl.multiple_of(n * WIDE, WIDE), WIDE)
            before = source[0][:, at].astype(f32) + source[1][:, at].astype(f32)
            after = before + dot_split((source[0][...], source[1][...]), (gram[0][:, at], gram[1][:, at]), NN)
            target[0][:, at], target[1][:, at] = split(after)
            return carry

        lax.fori_loop(0, columns // WIDE, chunk, 0)

    def correlate():
        for at in spans(size // LANES, LANES):
            a[at, at.start :] = dot_split((ph[at], plo[at]), (ph[at.start :], plo[at.start :]), NT)

    def rotate():
        for at in spans(size // LANES, LANES):
            turned = dot_split(split(x[at, : at.stop]), (ph[: at.stop], plo[: at.stop]), NN)
            qh[at], ql[at] = split(turned)

    lift((sh, sl), q)
    lift(q, p)
    correlate()
    inverse_factor(a, e, x, work)
    rotate()

    worst = jnp.zeros((), f32)
    for at in spans(size // LANES, LANES):
        gap = dot(qh[at], qh[...], NT)
        here = lax.broadcasted_iota(jnp.int32, gap.shape, 0) + at.start == lax.broadcasted_iota(jnp.int32, gap.shape, 1)
        gap = gap - here.astype(f32)
        worst = jnp.maximum(worst, jnp.max(jnp.sum(gap * gap, axis=1, keepdims=True)))

    @pl.when(jnp.logical_not(worst < ORTHO_TOL**2))
    def _():
        qh[...], ql[...] = sh[...], sl[...]

        def again(k, carry):
            turn = lax.rem(k, REPEAT)

            @pl.when(turn == 0)
            def _():
                lift(q, p)

            @pl.when(turn != 0)
            def _():
                ph[...], plo[...] = qh[...], ql[...]

            correlate()

            @pl.when(turn < 2)
            def _():
                eye = identity(LANES)
                tiles = [a[at, at] for at in spans(size // LANES, LANES)]
                shift = SHIFT * jnp.sum(sum(jnp.where(eye, tile, 0.0) for tile in tiles))
                for at, tile in zip(spans(size // LANES, LANES), tiles):
                    a[at, at] = tile + jnp.where(eye, shift, 0.0)

            inverse_factor(a, e, x, work)
            rotate()
            return carry

        lax.fori_loop(0, ITERS * REPEAT, again, 0)

    for lo in range(0, size, WIDE):
        modes[:, lo : lo + WIDE] = dot(rows[...], qh[lo : lo + WIDE], NT).astype(bf16)


def on_device(bases, start):
    local_rows, basis = bases.shape
    size = start.shape[1]
    n_batch, n_rows = lax.axis_size("batch"), lax.axis_size("rows")
    chips = n_rows // 2
    columns = basis * n_batch
    sub_rows = local_rows // n_batch
    per_basis = basis // LANES
    batch, row = lax.axis_index("batch"), lax.axis_index("rows")
    at = jnp.stack([row // 2, row % 2, batch]).astype(jnp.int32)
    tiles, share = tile_table(n_batch, per_basis, n_rows)
    table = jnp.asarray([k for tile in tiles for k in tile], jnp.int32)
    other_batches, other_chips = range(1, n_batch), range(2, n_rows, 2)

    def call(kernel, outs, scratch, *args, n_smem=0, flops=0, moved=1 << 20, after=()):
        def body(*refs):
            kernel(*refs[: len(args)], *refs[len(args) + len(after) :])

        return pl.pallas_call(
            body,
            out_shape=[jax.ShapeDtypeStruct(shape, dtype) for shape, dtype in outs],
            in_specs=[SMEM] * n_smem + [VMEM] * (len(args) - n_smem) + [ANY] * len(after),
            out_specs=[VMEM] * len(outs),
            scratch_shapes=[pltpu.VMEM(shape, dtype) for shape, dtype in scratch],
            compiler_params=pltpu.CompilerParams(vmem_limit_bytes=60 << 20),
            cost_estimate=pl.CostEstimate(flops=flops, bytes_accessed=moved, transcendentals=0),
        )(*args, *after)

    pieces = []
    for offset in range(n_batch):
        piece = lax.dynamic_slice_in_dim(bases, (batch ^ offset) * sub_rows, sub_rows, 0)
        pieces.append(swap(piece, "batch", offset) if offset else piece)
    other_pieces = [swap(piece, "rows", 1) for piece in pieces]

    own_count = len(own_tiles(per_basis))
    (diagonal,) = call(
        diagonal_kernel, [((own_count * LANES + SUB, LANES), f32)], [], bases,
        flops=2 * local_rows * own_count * LANES * LANES, moved=bases.size * 2, after=other_pieces[:1],
    )
    for offset in (1 << k for k in range(n_rows.bit_length() - 1)):
        diagonal = diagonal + swap(diagonal, "rows", offset)
    energy = diagonal[own_count * LANES :]
    for offset in (1 << k for k in range(n_batch.bit_length() - 1)):
        energy = energy + swap(energy, "batch", offset)
    scale = (SCALE * columns / jnp.sum(energy)).reshape(1)

    part = own_count * LANES // n_rows
    message_rows = part + start.size // n_rows // LANES
    rows, mine, *blocks = call(
        cross_kernel,
        [((sub_rows, columns), bf16), ((message_rows, LANES), f32)] + [((share * LANES, LANES), f32)] * chips,
        [((2 * sub_rows, columns), bf16)],
        at, table, scale, start, diagonal, *pieces, *other_pieces, n_smem=3,
        flops=4 * sub_rows * chips * share * LANES * LANES, moved=6 << 20,
    )
    plane = blocks[0]
    for block, offset in zip(blocks[1:], other_chips):
        plane = plane + swap(block.astype(f16), "rows", offset).astype(f32)
    plane = plane.astype(f16)
    total = plane.astype(f32)
    for offset in other_batches:
        total = total + swap(plane, "batch", offset).astype(f32)
    total = total.astype(f16)

    mine = spread_copy(mine, "batch", other_batches)
    mine = [mine] + [swap(mine, "rows", offset) for offset in other_chips]
    high, low, diagonal = call(
        prepare_kernel,
        [((size, columns), bf16)] * 2 + [((n_batch, own_count * LANES, LANES), f32)],
        [((columns, size), f32)],
        at, *mine, *(swap(block, "rows", 1) for block in mine), n_smem=1, moved=8 << 20,
    )

    cross = [total] + [swap(total, "rows", offset) for offset in other_chips]
    cross = jnp.stack(cross + [swap(block, "rows", 1) for block in cross]).astype(f32)
    (modes,) = call(
        solve_kernel,
        [((sub_rows, size), bf16)],
        [((columns, columns), bf16)] * 2
        + [((size, columns), bf16)] * 4
        + [((size, size), f32)] * 3
        + [((LANES, 2 * LANES), f32)],
        at, table, cross, diagonal, high, low, rows, n_smem=2, flops=10**10, moved=10 << 20,
    )
    return modes


def solution(mesh):
    in_specs = (P("rows", "batch"), P("batch", None))
    out_specs = P(("rows", "batch"), None)
    return jax.shard_map(
        on_device, mesh=mesh, in_specs=in_specs, out_specs=out_specs, check_vma=False
    )
```

```python
import functools

import jax
import jax.numpy as jnp
from jax import lax
from jax.experimental import pallas as pl
from jax.experimental.pallas import tpu as pltpu
from jax.sharding import PartitionSpec as P

ITERS = 2
LANES = 128
SUB = 8
PANEL = 32
REPEAT = 4
SHIFT = 2.0**-15
WIDE = 256
ORTHO_TOL = 2.0**-8
NN = ((1,), (0,))
TN = ((0,), (0,))
NT = ((1,), (1,))
f32 = jnp.float32
bf16 = jnp.bfloat16
f16 = jnp.float16
TOP = 14.0
VMEM = pl.BlockSpec(memory_space=pltpu.VMEM)
ANY = pl.BlockSpec(memory_space=pl.ANY)
SMEM = pl.BlockSpec(memory_space=pltpu.SMEM)


def dot(left, right, dims):
    return lax.dot_general(left, right, (dims, ((), ())), preferred_element_type=f32)


def split(value):
    high = value.astype(bf16)
    return high, (value - high.astype(f32)).astype(bf16)


def dot_split(left, right, dims):
    return dot(left[0], right[0], dims) + dot(left[0], right[1], dims) + dot(left[1], right[0], dims)


def swap(value, axis, offset):
    size = lax.axis_size(axis)
    return lax.ppermute(value, axis, [(i, i ^ offset) for i in range(size)])


def spans(count, size):
    return [slice(i * size, (i + 1) * size) for i in range(count)]


def tile_table(n_batch, per_basis, n_rows):
    tiles = [
        (first * per_basis + i, second * per_basis + j)
        for first in range(n_batch)
        for second in range(first + 1, n_batch)
        for i in range(per_basis)
        for j in range(per_basis)
    ]
    share = -(-len(tiles) // n_rows)
    return tiles + tiles[-1:] * (share * n_rows - len(tiles)), share


def own_tiles(per_basis):
    return [(i, j) for i in range(per_basis) for j in range(i, per_basis)]


def spread_copy(value, axis, offsets):
    return jnp.stack([value] + [swap(value, axis, offset) for offset in offsets])


def encode(value, power):
    return jnp.concatenate([value * jnp.exp2(TOP - power[:1]), power]).astype(f16)


def decode(coded):
    value, power = coded[:-SUB].astype(f32), coded[-SUB : 1 - SUB].astype(f32)
    return value * jnp.exp2(power - TOP)


def diagonal_kernel(bases, out):
    per_basis = bases.shape[1] // LANES
    columns = spans(per_basis, LANES)
    for at, (i, j) in zip(spans(len(own_tiles(per_basis)), LANES), own_tiles(per_basis)):
        out[at] = dot(bases[:, columns[i]], bases[:, columns[j]], TN)


def cross_kernel(at_ref, table, start, diagonal, *refs):
    n_batch = lax.axis_size("batch")
    pieces, (rows, message, *outs, both) = refs[: 2 * n_batch], refs[2 * n_batch :]
    chip, core, batch = at_ref[0], at_ref[1], at_ref[2]
    sub_rows, basis = pieces[0].shape
    for half in range(2):
        for offset in range(n_batch):
            first = pl.multiple_of(lax.bitwise_xor(batch, offset) * basis, basis)
            both[half * sub_rows : (half + 1) * sub_rows, pl.ds(first, basis)] = pieces[half * n_batch + offset][...]
    rows[...] = both[:sub_rows]
    index = 2 * chip + core
    share, size = start.shape[0] // lax.axis_size("rows"), start.shape[1]
    part = message.shape[0] - share * size // LANES
    message[:part] = diagonal[pl.ds(pl.multiple_of(index * part, SUB), part), :]
    for k, lanes in enumerate(spans(size // LANES, LANES)):
        first = pl.multiple_of(index * share, SUB)
        message[part + k * share : part + (k + 1) * share] = start[pl.ds(first, share), lanes]

    def add_squares(k, total):
        chunk = both[pl.ds(pl.multiple_of(k * LANES, LANES), LANES), :].astype(f32)
        chunk = chunk * chunk
        return total + sum(chunk[r, c] for r in spans(LANES // SUB, SUB) for c in spans(chunk.shape[1] // LANES, LANES))

    energy = lax.fori_loop(0, both.shape[0] // LANES, add_squares, jnp.zeros((SUB, LANES), f32))
    for offset, out in enumerate(outs):
        share = out.shape[0] // LANES
        out[share * LANES :] = energy
        owner = 2 * lax.bitwise_xor(chip, offset) + core
        for j, at in enumerate(spans(share, LANES)):
            place = 2 * (owner * share + j)
            left = pl.multiple_of(table[place] * LANES, LANES)
            right = pl.multiple_of(table[place + 1] * LANES, LANES)
            out[at] = dot(both[:, pl.ds(left, LANES)], both[:, pl.ds(right, LANES)], TN)


def spread(value, index):
    return jnp.broadcast_to(value[index : index + 1, :], value.shape)


def factor_block(work):
    groups = PANEL // SUB
    sub = lax.broadcasted_iota(jnp.int32, (SUB, LANES), 0)
    for r0 in range(0, LANES, PANEL):
        m = [
            [work[r0 + SUB * g : r0 + SUB * (g + 1), LANES * t : LANES * (t + 1)] for t in range(2)]
            for g in range(groups)
        ]
        col = {}
        for j in range(PANEL):
            for g in range(j // SUB, groups):
                col[j, g] = jnp.broadcast_to(m[g][0][:, r0 + j : r0 + j + 1], (SUB, LANES))
        scale = [None] * groups
        for j in range(PANEL):
            gj, sj = divmod(j, SUB)
            pivot = spread(col[j, gj], sj)
            inverse = 1.0 / pivot
            root = lax.rsqrt(pivot)
            scale[gj] = root if scale[gj] is None else jnp.where(sub == sj, root, scale[gj])
            source = [spread(m[gj][t], sj) for t in range(2)]
            scaled = {g: col[j, g] * inverse for g in range(gj, groups)}
            for k in range(j + 1, PANEL):
                entry = spread(col[j, k // SUB], k % SUB)
                for g in range(k // SUB, groups):
                    col[k, g] = col[k, g] - scaled[g] * entry
            for g in range(gj, groups):
                factor = jnp.where(sub > sj, scaled[g], 0.0) if g == gj else scaled[g]
                for t in range(2):
                    m[g][t] = m[g][t] - factor * source[t]
        rows = jnp.concatenate(
            [jnp.concatenate([m[g][t] * scale[g] for t in range(2)], axis=1) for g in range(groups)], axis=0
        )
        work[r0 : r0 + PANEL, :] = rows
        below = r0 + PANEL
        if below < LANES:
            high, low = split(rows)
            left = jnp.concatenate([high[:, :LANES], high[:, :LANES], low[:, :LANES]], axis=0)
            right = jnp.concatenate([high, low, high], axis=0)
            work[below:, :] = work[below:, :] - dot(left, right, TN)[below:, :]


def identity(size):
    return lax.broadcasted_iota(jnp.int32, (size, size), 0) == lax.broadcasted_iota(jnp.int32, (size, size), 1)


def inverse_factor(a, e, x, work):
    size = a.shape[0]
    e[...] = identity(size).astype(f32)
    lanes = lax.broadcasted_iota(jnp.int32, (LANES, size), 1)

    def block(k, carry):
        at = pl.ds(pl.multiple_of(k * LANES, LANES), LANES)
        work[:, :LANES] = a[at, at]
        work[:, LANES:] = identity(LANES).astype(f32)
        factor_block(work)
        own = split(work[:, LANES:])
        x_rows = dot_split(own, split(e[at, :]), NN)
        x[at, :] = x_rows
        upper = dot_split(own, split(a[at, :]), NN)
        upper = split(jnp.where(lanes >= (k + 1) * LANES, upper, 0.0))
        a[...] = a[...] - dot_split(upper, upper, TN)
        e[...] = e[...] - dot_split(upper, split(x_rows), TN)
        return carry

    lax.fori_loop(0, size // LANES, block, 0)


def prepare_kernel(at_ref, *refs):
    *blocks, high, low, diagonal, whole = refs
    chip, core, batch = at_ref[0], at_ref[1], at_ref[2]
    n_batch = blocks[0].shape[0]
    columns, size = whole.shape
    basis = columns // n_batch
    share = basis // len(blocks)
    part = diagonal.shape[1] // len(blocks)
    for k, block in enumerate(blocks):
        other, offset = divmod(k, len(blocks) // 2)
        row = 2 * lax.bitwise_xor(chip, offset) + lax.bitwise_xor(core, other)
        for z in range(n_batch):
            group = lax.bitwise_xor(batch, z)
            diagonal[group, pl.ds(pl.multiple_of(row * part, SUB), part), :] = block[z, :part, :]
            first = pl.multiple_of(group * basis + row * share, SUB)
            for k, lanes in enumerate(spans(size // LANES, LANES)):
                lower = part + k * share
                whole[pl.ds(first, share), lanes] = block[z, lower : lower + share, :]
    for rows in spans(columns // LANES, LANES):
        high[:, rows], low[:, rows] = split(whole[rows, :].T)


def trace_of(diagonal, per_basis):
    total = jnp.zeros((LANES, LANES), f32)
    eye = identity(LANES)
    for group in range(diagonal.shape[0]):
        for at, (i, j) in zip(spans(len(own_tiles(per_basis)), LANES), own_tiles(per_basis)):
            if i == j:
                total = total + jnp.where(eye, diagonal[group, at, :], 0.0)
    return jnp.sum(total)


def place_gram(at_ref, table, cross, diagonal, factor, pair):
    chip, core = at_ref[0], at_ref[1]
    devices, share_rows, _ = cross.shape
    share = share_rows // LANES
    n_batch = diagonal.shape[0]
    per_basis = pair[0].shape[0] // LANES // n_batch

    def place(k, carry):
        other, offset = k // (devices // 2), lax.rem(k, devices // 2)
        owner = 2 * lax.bitwise_xor(chip, offset) + lax.bitwise_xor(core, other)
        unit = jnp.exp2(cross[k, share * LANES : share * LANES + 1, :] - TOP) * factor
        for j, inner in enumerate(spans(share, LANES)):
            at = 2 * (owner * share + j)
            row = pl.ds(pl.multiple_of(table[at] * LANES, LANES), LANES)
            column = pl.ds(pl.multiple_of(table[at + 1] * LANES, LANES), LANES)
            for ref, value in zip(pair, split(cross[k, inner, :] * unit)):
                ref[row, column] = value
                ref[column, row] = value.T
        return carry

    lax.fori_loop(0, devices, place, 0)
    for group in range(n_batch):
        for at, (i, j) in zip(spans(len(own_tiles(per_basis)), LANES), own_tiles(per_basis)):
            rows, columns = (slice((group * per_basis + k) * LANES, (group * per_basis + k + 1) * LANES) for k in (i, j))
            for ref, value in zip(pair, split(diagonal[group, at, :] * factor)):
                ref[rows, columns] = value
                if i != j:
                    ref[columns, rows] = value.T


def solve_kernel(at_ref, table, cross, diagonal, sh, sl, rows, modes, ah, al, ph, plo, qh, ql, a, e, x, work):
    size, columns = sh.shape
    per_basis = columns // LANES // diagonal.shape[0]
    gram, p, q = (ah, al), (ph, plo), (qh, ql)
    factor = 1.0 / (trace_of(diagonal, per_basis) / columns)
    place_gram(at_ref, table, cross, diagonal, factor, gram)

    def lift(source, target):
        def chunk(n, carry):
            at = pl.ds(pl.multiple_of(n * WIDE, WIDE), WIDE)
            before = source[0][:, at].astype(f32) + source[1][:, at].astype(f32)
            after = before + dot_split((source[0][...], source[1][...]), (gram[0][:, at], gram[1][:, at]), NN)
            target[0][:, at], target[1][:, at] = split(after)
            return carry

        lax.fori_loop(0, columns // WIDE, chunk, 0)

    def correlate():
        for at in spans(size // LANES, LANES):
            a[at, at.start :] = dot_split((ph[at], plo[at]), (ph[at.start :], plo[at.start :]), NT)

    def rotate():
        for at in spans(size // LANES, LANES):
            turned = dot_split(split(x[at, : at.stop]), (ph[: at.stop], plo[: at.stop]), NN)
            qh[at], ql[at] = split(turned)

    lift((sh, sl), q)
    lift(q, p)
    correlate()
    inverse_factor(a, e, x, work)
    rotate()

    worst = jnp.zeros((), f32)
    for at in spans(size // LANES, LANES):
        gap = dot(qh[at], qh[...], NT)
        here = lax.broadcasted_iota(jnp.int32, gap.shape, 0) + at.start == lax.broadcasted_iota(jnp.int32, gap.shape, 1)
        gap = gap - here.astype(f32)
        worst = jnp.maximum(worst, jnp.max(jnp.sum(gap * gap, axis=1, keepdims=True)))

    @pl.when(jnp.logical_not(worst < ORTHO_TOL**2))
    def _():
        qh[...], ql[...] = sh[...], sl[...]

        def again(k, carry):
            turn = lax.rem(k, REPEAT)

            @pl.when(turn == 0)
            def _():
                lift(q, p)

            @pl.when(turn != 0)
            def _():
                ph[...], plo[...] = qh[...], ql[...]

            correlate()

            @pl.when(turn < 2)
            def _():
                eye = identity(LANES)
                tiles = [a[at, at] for at in spans(size // LANES, LANES)]
                shift = SHIFT * jnp.sum(sum(jnp.where(eye, tile, 0.0) for tile in tiles))
                for at, tile in zip(spans(size // LANES, LANES), tiles):
                    a[at, at] = tile + jnp.where(eye, shift, 0.0)

            inverse_factor(a, e, x, work)
            rotate()
            return carry

        lax.fori_loop(0, ITERS * REPEAT, again, 0)

    for lo in range(0, size, WIDE):
        modes[:, lo : lo + WIDE] = dot(rows[...], qh[lo : lo + WIDE], NT).astype(bf16)


def on_device(bases, start):
    local_rows, basis = bases.shape
    size = start.shape[1]
    n_batch, n_rows = lax.axis_size("batch"), lax.axis_size("rows")
    chips = n_rows // 2
    columns = basis * n_batch
    sub_rows = local_rows // n_batch
    per_basis = basis // LANES
    batch, row = lax.axis_index("batch"), lax.axis_index("rows")
    at = jnp.stack([row // 2, row % 2, batch]).astype(jnp.int32)
    tiles, share = tile_table(n_batch, per_basis, n_rows)
    table = jnp.asarray([k for tile in tiles for k in tile], jnp.int32)
    other_batches, other_chips = range(1, n_batch), range(2, n_rows, 2)

    def call(kernel, outs, scratch, *args, n_smem=0, flops=0, moved=1 << 20, after=()):
        def body(*refs):
            kernel(*refs[: len(args)], *refs[len(args) + len(after) :])

        return pl.pallas_call(
            body,
            out_shape=[jax.ShapeDtypeStruct(shape, dtype) for shape, dtype in outs],
            in_specs=[SMEM] * n_smem + [VMEM] * (len(args) - n_smem) + [ANY] * len(after),
            out_specs=[VMEM] * len(outs),
            scratch_shapes=[pltpu.VMEM(shape, dtype) for shape, dtype in scratch],
            compiler_params=pltpu.CompilerParams(vmem_limit_bytes=60 << 20),
            cost_estimate=pl.CostEstimate(flops=flops, bytes_accessed=moved, transcendentals=0),
        )(*args, *after)

    pieces = []
    for offset in range(n_batch):
        piece = lax.dynamic_slice_in_dim(bases, (batch ^ offset) * sub_rows, sub_rows, 0)
        pieces.append(swap(piece, "batch", offset) if offset else piece)
    other_pieces = [swap(piece, "rows", 1) for piece in pieces]

    own_count = len(own_tiles(per_basis))
    (diagonal,) = call(
        diagonal_kernel, [((own_count * LANES, LANES), f32)], [], bases,
        flops=2 * local_rows * own_count * LANES * LANES, moved=bases.size * 2, after=other_pieces[:1],
    )
    diagonal = diagonal + swap(diagonal, "rows", 1)
    diagonal = sum((swap(diagonal, "rows", offset) for offset in other_chips), diagonal)

    part = own_count * LANES // n_rows
    message_rows = part + start.size // n_rows // LANES
    tile_rows = share * LANES
    rows, mine, *blocks = call(
        cross_kernel,
        [((sub_rows, columns), bf16), ((message_rows, LANES), f32)] + [((tile_rows + SUB, LANES), f32)] * chips,
        [((2 * sub_rows, columns), bf16)],
        at, table, start, diagonal, *pieces, *other_pieces, n_smem=2,
        flops=4 * sub_rows * chips * share * LANES * LANES, moved=6 << 20,
    )
    plane = sum((swap(block, "rows", offset) for block, offset in zip(blocks[1:], other_chips)), blocks[0])
    power = jnp.floor(jnp.log2(jnp.sum(plane[tile_rows:]))) + 1
    power = jnp.full((SUB, LANES), power, f32)
    plane = encode(plane[:tile_rows], power)
    planes = [plane] + [swap(plane, "batch", offset) for offset in other_batches]
    total = sum(decode(value) for value in planes)
    power = jnp.ceil(jnp.log2(sum(jnp.exp2(value[tile_rows:].astype(f32)) for value in planes)))
    total = encode(total, power)

    mine = spread_copy(mine, "batch", other_batches)
    mine = [mine] + [swap(mine, "rows", offset) for offset in other_chips]
    total, mine = lax.optimization_barrier((total, mine))
    high, low, diagonal = call(
        prepare_kernel,
        [((size, columns), bf16)] * 2 + [((n_batch, own_count * LANES, LANES), f32)],
        [((columns, size), f32)],
        at, *mine, *(swap(block, "rows", 1) for block in mine), n_smem=1, moved=8 << 20,
    )

    cross = spread_copy(total, "rows", other_chips)
    cross = jnp.concatenate([cross, swap(cross, "rows", 1)]).astype(f32)
    (modes,) = call(
        solve_kernel,
        [((sub_rows, size), bf16)],
        [((columns, columns), bf16)] * 2
        + [((size, columns), bf16)] * 4
        + [((size, size), f32)] * 3
        + [((LANES, 2 * LANES), f32)],
        at, table, cross, diagonal, high, low, rows, n_smem=2, flops=10**10, moved=10 << 20,
    )
    return modes


def solution(mesh):
    in_specs = (P("rows", "batch"), P("batch", None))
    out_specs = P(("rows", "batch"), None)
    return jax.shard_map(
        on_device, mesh=mesh, in_specs=in_specs, out_specs=out_specs, check_vma=False
    )
```

```python
import functools
import math

import jax
import jax.numpy as jnp
from jax import lax
from jax.experimental import pallas as pl
from jax.experimental.pallas import tpu as pltpu
from jax.sharding import PartitionSpec as P

ITERS = 2
LANES = 128
SUB = 8
PANEL = 32
REPEAT = 4
SHIFT = 2.0**-15
WIDE = 512
ORTHO_TOL = 2.0**-8
NN = ((1,), (0,))
TN = ((0,), (0,))
NT = ((1,), (1,))
f32 = jnp.float32
bf16 = jnp.bfloat16
f16 = jnp.float16
TOP = 14.0
TINY = 2.0**-100
VMEM = pl.BlockSpec(memory_space=pltpu.VMEM)
ANY = pl.BlockSpec(memory_space=pl.ANY)
SMEM = pl.BlockSpec(memory_space=pltpu.SMEM)


def dot(left, right, dims):
    return lax.dot_general(left, right, (dims, ((), ())), preferred_element_type=f32)


def split(value):
    high = value.astype(bf16)
    return high, (value - high.astype(f32)).astype(bf16)


def dot_split(left, right, dims):
    (k_left,), (k_right,) = dims
    return dot(
        jnp.concatenate([left[0], left[0], left[1]], axis=k_left),
        jnp.concatenate([right[0], right[1], right[0]], axis=k_right),
        dims,
    )


def swap(value, axis, offset):
    size = lax.axis_size(axis)
    return lax.ppermute(value, axis, [(i, i ^ offset) for i in range(size)])


def spans(count, size):
    return [slice(i * size, (i + 1) * size) for i in range(count)]


def tile_table(n_batch, per_basis, n_rows):
    tiles = [
        (first * per_basis + i, second * per_basis + j)
        for first in range(n_batch)
        for second in range(first + 1, n_batch)
        for i in range(per_basis)
        for j in range(per_basis)
    ]
    share = -(-len(tiles) // n_rows)
    return tiles + tiles[-1:] * (share * n_rows - len(tiles)), share


def own_tiles(per_basis):
    return [(i, j) for i in range(per_basis) for j in range(i, per_basis)]


def spread_copy(value, axis, offsets):
    return jnp.stack([value] + [swap(value, axis, offset) for offset in offsets])


def encode(value):
    power = jnp.floor(jnp.log2(jnp.maximum(value[-SUB:], TINY))) + 1
    scaled = value[:-SUB].reshape(-1, SUB, LANES) * jnp.exp2(TOP - power)
    return jnp.concatenate([scaled.reshape(-1, LANES), power]).astype(f16)


def decode(coded):
    value = coded.astype(f32)
    bound = jnp.exp2(value[-SUB:])
    scaled = value[:-SUB].reshape(-1, SUB, LANES) * (bound * 2.0**-TOP)
    return jnp.concatenate([scaled.reshape(-1, LANES), bound])


def largest(value):
    groups = [jnp.abs(value[rows]) for rows in spans(value.shape[0] // SUB, SUB)]
    return functools.reduce(jnp.maximum, groups)


def diagonal_kernel(bases, out):
    per_basis = bases.shape[1] // LANES
    columns = spans(per_basis, LANES)
    for at, (i, j) in zip(spans(len(own_tiles(per_basis)), LANES), own_tiles(per_basis)):
        out[at] = dot(bases[:, columns[i]], bases[:, columns[j]], TN)


def cross_kernel(at_ref, table, start, diagonal, *refs):
    n_batch = lax.axis_size("batch")
    pieces, (rows, message, *outs, both) = refs[: 2 * n_batch], refs[2 * n_batch :]
    chip, core, batch = at_ref[0], at_ref[1], at_ref[2]
    sub_rows, basis = pieces[0].shape
    for half in range(2):
        for offset in range(n_batch):
            first = pl.multiple_of(lax.bitwise_xor(batch, offset) * basis, basis)
            both[half * sub_rows : (half + 1) * sub_rows, pl.ds(first, basis)] = pieces[half * n_batch + offset][...]
    rows[...] = both[:sub_rows]
    index = 2 * chip + core
    share, size = start.shape[0] // lax.axis_size("rows"), start.shape[1]
    part = message.shape[0] - share * size // LANES - 2 * SUB
    message[:part] = diagonal[pl.ds(pl.multiple_of(index * part, SUB), part), :]
    message[part : part + SUB] = largest(message[:part])
    lower = part + SUB
    for k, lanes in enumerate(spans(size // LANES, LANES)):
        first = pl.multiple_of(index * share, SUB)
        message[lower + k * share : lower + (k + 1) * share] = start[pl.ds(first, share), lanes]
    message[lower + size // LANES * share :] = largest(message[lower : lower + size // LANES * share])
    for offset, out in enumerate(outs):
        share = out.shape[0] // LANES
        owner = 2 * lax.bitwise_xor(chip, offset) + core
        bound = jnp.zeros((SUB, LANES), f32)
        for j, at in enumerate(spans(share, LANES)):
            place = 2 * (owner * share + j)
            left = pl.multiple_of(table[place] * LANES, LANES)
            right = pl.multiple_of(table[place + 1] * LANES, LANES)
            tile = dot(both[:, pl.ds(left, LANES)], both[:, pl.ds(right, LANES)], TN)
            out[at] = tile
            bound = jnp.maximum(bound, largest(tile))
        out[share * LANES :] = bound


def spread(value, index):
    return jnp.broadcast_to(value[index : index + 1, :], value.shape)


def factor_block(work, background=()):
    background = list(background)
    groups = PANEL // SUB
    sub = lax.broadcasted_iota(jnp.int32, (SUB, LANES), 0)
    for r0 in range(0, LANES, PANEL):
        m = [
            [work[r0 + SUB * g : r0 + SUB * (g + 1), LANES * t : LANES * (t + 1)] for t in range(2)]
            for g in range(groups)
        ]
        col = {}
        for j in range(PANEL):
            for g in range(j // SUB, groups):
                col[j, g] = jnp.broadcast_to(m[g][0][:, r0 + j : r0 + j + 1], (SUB, LANES))
        scale = [None] * groups
        pivot = spread(col[0, 0], 0)
        for j in range(PANEL):
            gj, sj = divmod(j, SUB)
            inverse = 1.0 / pivot
            root = lax.rsqrt(pivot)
            if j + 1 < PANEL:
                g, k = divmod(j + 1, SUB)
                entry = spread(col[j, g], k)
                pivot = spread(col[j + 1, g], k) - entry * entry * inverse
            if background and j % 8 == 4:
                background.pop(0)()
            scale[gj] = root if scale[gj] is None else jnp.where(sub == sj, root, scale[gj])
            source = [spread(m[gj][t], sj) for t in range(2)]
            scaled = {g: col[j, g] * inverse for g in range(gj, groups)}
            for k in range(j + 1, PANEL):
                entry = spread(col[j, k // SUB], k % SUB)
                for g in range(k // SUB, groups):
                    col[k, g] = col[k, g] - scaled[g] * entry
            for g in range(gj, groups):
                factor = jnp.where(sub > sj, scaled[g], 0.0) if g == gj else scaled[g]
                for t in range(2):
                    m[g][t] = m[g][t] - factor * source[t]
        rows = jnp.concatenate(
            [jnp.concatenate([m[g][t] * scale[g] for t in range(2)], axis=1) for g in range(groups)], axis=0
        )
        work[r0 : r0 + PANEL, :] = rows
        below = r0 + PANEL
        if below < LANES:
            high, low = split(rows)
            left = jnp.concatenate([high[:, :LANES], high[:, :LANES], low[:, :LANES]], axis=0)
            right = jnp.concatenate([high, low, high], axis=0)
            work[below:, :] = work[below:, :] - dot(left, right, TN)[below:, :]


def identity(size):
    return lax.broadcasted_iota(jnp.int32, (size, size), 0) == lax.broadcasted_iota(jnp.int32, (size, size), 1)


def pair_of(ref, *at):
    return ref[0, *at], ref[1, *at]


def orthonormal_rows(a, rest, upper, work, out):
    size = a.shape[0]
    blocks = size // LANES
    lanes = lax.broadcasted_iota(jnp.int32, (LANES, size), 1)
    upper[...] = jnp.zeros(upper.shape, bf16)

    def block(k, carry):
        at = pl.ds(pl.multiple_of(k * LANES, LANES), LANES)
        last = pl.ds(pl.multiple_of(jnp.maximum(k - 1, 0) * LANES, LANES), LANES)
        following = pl.ds(pl.multiple_of(jnp.minimum(k + 1, blocks - 1) * LANES, LANES), LANES)
        work[:, :LANES] = a[at, at]
        work[:, LANES:] = identity(LANES).astype(f32)
        before = pair_of(upper)
        later = [jnp.where(lanes >= (k + 1) * LANES, part.astype(f32), 0.0).astype(bf16) for part in before]
        known = pair_of(out, last)

        def update(ref, rows, left, right):
            left = [part[:, rows] for part in left]
            ref[rows] = ref[rows] - dot_split(left, right, TN)

        background = [
            functools.partial(update, ref, rows, left, right)
            for ref, left, right in ((a, later, before), (rest, before, known))
            for rows in spans(blocks, LANES)
        ]
        factor_block(work, background)
        own = split(work[:, LANES:])
        rows = dot_split(own, split(a[at, :]), NN)
        upper[0], upper[1] = split(jnp.where(lanes >= (k + 1) * LANES, rows, 0.0))
        out[0, at], out[1, at] = split(dot_split(own, split(rest[at, :]), NN))
        a[following, :] = a[following, :] - dot_split(pair_of(upper, slice(None), following), pair_of(upper), TN)
        return carry

    lax.fori_loop(0, blocks, block, 0)


def prepare_kernel(at_ref, *refs):
    *blocks, high, low, diagonal, whole = refs
    chip, core, batch = at_ref[0], at_ref[1], at_ref[2]
    n_batch = blocks[0].shape[0]
    columns, size = whole.shape
    basis = columns // n_batch
    share = basis // len(blocks)
    part = diagonal.shape[1] // len(blocks)
    for k, block in enumerate(blocks):
        other, offset = divmod(k, len(blocks) // 2)
        row = 2 * lax.bitwise_xor(chip, offset) + lax.bitwise_xor(core, other)
        for z in range(n_batch):
            group = lax.bitwise_xor(batch, z)
            diagonal[group, pl.ds(pl.multiple_of(row * part, SUB), part), :] = block[z, :part, :]
            first = pl.multiple_of(group * basis + row * share, SUB)
            for k, lanes in enumerate(spans(size // LANES, LANES)):
                lower = part + SUB + k * share
                whole[pl.ds(first, share), lanes] = block[z, lower : lower + share, :]
    for rows in spans(columns // LANES, LANES):
        high[:, rows], low[:, rows] = split(whole[rows, :].T)


def trace_of(diagonal, per_basis):
    total = jnp.zeros((LANES, LANES), f32)
    eye = identity(LANES)
    for group in range(diagonal.shape[0]):
        for at, (i, j) in zip(spans(len(own_tiles(per_basis)), LANES), own_tiles(per_basis)):
            if i == j:
                total = total + jnp.where(eye, diagonal[group, at, :], 0.0)
    return jnp.sum(total)


def place_gram(at_ref, table, cross, diagonal, factor, pair):
    chip, core = at_ref[0], at_ref[1]
    devices, share_rows, _ = cross.shape
    share = share_rows // LANES
    n_batch = diagonal.shape[0]
    per_basis = pair[0].shape[0] // LANES // n_batch

    def place(k, carry):
        other, offset = k // (devices // 2), lax.rem(k, devices // 2)
        owner = 2 * lax.bitwise_xor(chip, offset) + lax.bitwise_xor(core, other)
        for j, inner in enumerate(spans(share, LANES)):
            at = 2 * (owner * share + j)
            row = pl.ds(pl.multiple_of(table[at] * LANES, LANES), LANES)
            column = pl.ds(pl.multiple_of(table[at + 1] * LANES, LANES), LANES)
            tile = cross[k, inner, :] * factor
            pair[0][row, column], pair[1][row, column] = split(tile)
            pair[0][column, row], pair[1][column, row] = split(tile.T)
        return carry

    lax.fori_loop(0, devices, place, 0)
    for group in range(n_batch):
        for at, (i, j) in zip(spans(len(own_tiles(per_basis)), LANES), own_tiles(per_basis)):
            rows, columns = (slice((group * per_basis + k) * LANES, (group * per_basis + k + 1) * LANES) for k in (i, j))
            for ref, value in zip(pair, split(diagonal[group, at, :] * factor)):
                ref[rows, columns] = value
                if i != j:
                    ref[columns, rows] = value.T


def solve_kernel(at_ref, table, cross, diagonal, sh, sl, rows, modes, ah, al, lifted, q, a, rest, upper, work):
    size, columns = sh.shape
    per_basis = columns // LANES // diagonal.shape[0]
    gram = (ah, al)
    factor = 1.0 / (trace_of(diagonal, per_basis) / columns)
    place_gram(at_ref, table, cross, diagonal, factor, gram)

    def lift(source, target):
        left = pair_of(source)

        def chunk(n, carry):
            at = pl.ds(pl.multiple_of(n * WIDE, WIDE), WIDE)
            before = source[0, :, at].astype(f32) + source[1, :, at].astype(f32)
            after = before + dot_split(left, (gram[0][:, at], gram[1][:, at]), NN)
            rest[:, at] = after
            target[0, :, at], target[1, :, at] = split(after)
            return carry

        lax.fori_loop(0, columns // WIDE, chunk, 0)

    def turn_of(step):
        return lax.rem(step + REPEAT - 1, REPEAT)

    def normalise(carry):
        step, failed = carry
        turn = turn_of(step)

        @pl.when(step < 2)
        def _():
            q[0], q[1] = sh[...], sl[...]

        @pl.when(step == 0)
        def _():
            lift(q, lifted)
            q[...] = lifted[...]

        @pl.when((step == 0) | (turn == 0))
        def _():
            lift(q, lifted)

        @pl.when((step != 0) & (turn != 0))
        def _():
            lifted[...] = q[...]
            rest[...] = q[0].astype(f32) + q[1].astype(f32)

        for at in spans(size // (2 * LANES), 2 * LANES):
            a[at, at.start :] = dot_split(pair_of(lifted, at), pair_of(lifted, slice(at.start, None)), NT)

        @pl.when((step != 0) & (turn < 2))
        def _():
            eye = identity(LANES)
            tiles = [a[at, at] for at in spans(size // LANES, LANES)]
            shift = SHIFT * jnp.sum(sum(jnp.where(eye, tile, 0.0) for tile in tiles))
            for at, tile in zip(spans(size // LANES, LANES), tiles):
                a[at, at] = tile + jnp.where(eye, shift, 0.0)

        orthonormal_rows(a, rest, upper, work, q)

        worst = jnp.zeros((LANES, 1), f32)
        for at in spans(size // LANES, LANES):
            gap = dot(q[0, at], q[0], NT)
            here = lax.broadcasted_iota(jnp.int32, gap.shape, 0) + at.start == lax.broadcasted_iota(jnp.int32, gap.shape, 1)
            gap = gap - here.astype(f32)
            worst = jnp.maximum(worst, jnp.sum(gap * gap, axis=1, keepdims=True))
        worst = jnp.max(worst)
        for at in spans(size // WIDE, WIDE):
            modes[:, at] = dot(rows[...], q[0, at], NT).astype(bf16)
        good = worst < ORTHO_TOL**2
        return step + 1, jnp.where((step == 0) & good, 0, failed)

    lax.while_loop(
        lambda carry: (carry[0] == 0) | ((carry[1] == 1) & (carry[0] <= ITERS * REPEAT)),
        normalise,
        (jnp.int32(0), jnp.int32(1)),
    )


def scratch_of(size, columns):
    return (
        [((columns, columns), bf16)] * 2
        + [((2, size, columns), bf16)] * 2
        + [((size, size), f32), ((size, columns), f32), ((2, LANES, size), bf16), ((LANES, 2 * LANES), f32)]
    )


def on_device(bases, start):
    local_rows, basis = bases.shape
    size = start.shape[1]
    n_batch, n_rows = lax.axis_size("batch"), lax.axis_size("rows")
    chips = n_rows // 2
    columns = basis * n_batch
    sub_rows = local_rows // n_batch
    per_basis = basis // LANES
    batch, row = lax.axis_index("batch"), lax.axis_index("rows")
    at = jnp.stack([row // 2, row % 2, batch]).astype(jnp.int32)
    tiles, share = tile_table(n_batch, per_basis, n_rows)
    table = jnp.asarray([k for tile in tiles for k in tile], jnp.int32)
    other_batches, other_chips = range(1, n_batch), range(2, n_rows, 2)

    def call(kernel, outs, scratch, *args, n_smem=0, flops=0, moved=1 << 20, after=()):
        def body(*refs):
            kernel(*refs[: len(args)], *refs[len(args) + len(after) :])

        held = [(a.shape, a.dtype) for a in args] + outs + scratch
        room = sum(math.prod(shape) * jnp.dtype(dtype).itemsize for shape, dtype in held)
        return pl.pallas_call(
            body,
            out_shape=[jax.ShapeDtypeStruct(shape, dtype) for shape, dtype in outs],
            in_specs=[SMEM] * n_smem + [VMEM] * (len(args) - n_smem) + [ANY] * len(after),
            out_specs=[VMEM] * len(outs),
            scratch_shapes=[pltpu.VMEM(shape, dtype) for shape, dtype in scratch],
            compiler_params=pltpu.CompilerParams(vmem_limit_bytes=(6 << 20) + room),
            cost_estimate=pl.CostEstimate(flops=flops, bytes_accessed=moved, transcendentals=0),
        )(*args, *after)

    pieces = []
    for offset in range(n_batch):
        piece = lax.dynamic_slice_in_dim(bases, (batch ^ offset) * sub_rows, sub_rows, 0)
        pieces.append(swap(piece, "batch", offset) if offset else piece)
    other_pieces = [swap(piece, "rows", 1) for piece in pieces]

    own_count = len(own_tiles(per_basis))
    (diagonal,) = call(
        diagonal_kernel, [((own_count * LANES, LANES), f32)], [], bases,
        flops=2 * local_rows * own_count * LANES * LANES, moved=bases.size * 2, after=other_pieces[:1],
    )
    diagonal = diagonal + swap(diagonal, "rows", 1)
    diagonal = sum((swap(diagonal, "rows", offset) for offset in other_chips), diagonal)

    part = own_count * LANES // n_rows
    message_rows = part + start.size // n_rows // LANES + 2 * SUB
    tile_rows = share * LANES
    rows, mine, *blocks = call(
        cross_kernel,
        [((sub_rows, columns), bf16), ((message_rows, LANES), f32)] + [((tile_rows + SUB, LANES), f32)] * chips,
        [((2 * sub_rows, columns), bf16)],
        at, table, start, diagonal, *pieces, *other_pieces, n_smem=2,
        flops=4 * sub_rows * chips * share * LANES * LANES, moved=6 << 20,
    )
    plane = sum((swap(block, "rows", offset) for block, offset in zip(blocks[1:], other_chips)), blocks[0])
    planes = encode(plane)
    planes = [planes] + [swap(planes, "batch", offset) for offset in other_batches]
    total = encode(sum(decode(value) for value in planes))

    mine = jnp.concatenate([encode(mine[: part + SUB]), encode(mine[part + SUB :])])
    mine = spread_copy(mine, "batch", other_batches)
    mine = [mine] + [swap(mine, "rows", offset) for offset in other_chips]
    total, mine = lax.optimization_barrier((total, mine))

    def decode_message(blocks):
        return jnp.stack([jnp.concatenate([decode(b[: part + SUB]), decode(b[part + SUB :])]) for b in blocks])

    high, low, diagonal = call(
        prepare_kernel,
        [((size, columns), bf16)] * 2 + [((n_batch, own_count * LANES, LANES), f32)],
        [((columns, size), f32)],
        at, *map(decode_message, mine + [swap(block, "rows", 1) for block in mine]), n_smem=1, moved=8 << 20,
    )

    cross = spread_copy(total, "rows", other_chips)
    cross, high, low, diagonal = lax.optimization_barrier((cross, high, low, diagonal))
    cross = jnp.concatenate([cross, swap(cross, "rows", 1)])
    cross = jax.vmap(decode)(cross)
    (modes,) = call(
        solve_kernel,
        [((sub_rows, size), bf16)],
        scratch_of(size, columns),
        at, table, cross, diagonal, high, low, rows, n_smem=2, flops=10**10, moved=10 << 20,
    )
    return modes


def solution(mesh):
    in_specs = (P("rows", "batch"), P("batch", None))
    out_specs = P(("rows", "batch"), None)
    return jax.shard_map(
        on_device, mesh=mesh, in_specs=in_specs, out_specs=out_specs, check_vma=False
    )
```

```python
import functools
import math

import jax
import jax.numpy as jnp
from jax import lax
from jax.experimental import pallas as pl
from jax.experimental.pallas import tpu as pltpu
from jax.sharding import PartitionSpec as P

ITERS = 2
LANES = 128
SUB = 8
PANEL = 32
STEP = 16
REPEAT = 4
SHIFT = 2.0**-15
WIDE = 512
ORTHO_TOL = 2.0**-8
NN = ((1,), (0,))
TN = ((0,), (0,))
NT = ((1,), (1,))
f32 = jnp.float32
bf16 = jnp.bfloat16
f16 = jnp.float16
TOP = 14.0
TINY = 2.0**-100
VMEM = pl.BlockSpec(memory_space=pltpu.VMEM)
ANY = pl.BlockSpec(memory_space=pl.ANY)
SMEM = pl.BlockSpec(memory_space=pltpu.SMEM)


def dot(left, right, dims):
    return lax.dot_general(left, right, (dims, ((), ())), preferred_element_type=f32)


def split(value):
    high = value.astype(bf16)
    return high, (value - high.astype(f32)).astype(bf16)


def dot_split(left, right, dims):
    (k_left,), (k_right,) = dims
    return dot(
        jnp.concatenate([left[0], left[0], left[1]], axis=k_left),
        jnp.concatenate([right[0], right[1], right[0]], axis=k_right),
        dims,
    )


def swap(value, axis, offset):
    size = lax.axis_size(axis)
    return lax.ppermute(value, axis, [(i, i ^ offset) for i in range(size)])


def spans(count, size):
    return [slice(i * size, (i + 1) * size) for i in range(count)]


def tile_table(n_batch, per_basis, n_rows):
    tiles = [
        (first * per_basis + i, second * per_basis + j)
        for first in range(n_batch)
        for second in range(first + 1, n_batch)
        for i in range(per_basis)
        for j in range(per_basis)
    ]
    share = -(-len(tiles) // n_rows)
    return tiles + tiles[-1:] * (share * n_rows - len(tiles)), share


def own_tiles(per_basis):
    return [(i, j) for i in range(per_basis) for j in range(i, per_basis)]


def spread_copy(value, axis, offsets):
    return jnp.stack([value] + [swap(value, axis, offset) for offset in offsets])


def encode(value):
    power = jnp.floor(jnp.log2(jnp.maximum(value[-SUB:], TINY))) + 1
    scaled = value[:-SUB].reshape(-1, SUB, LANES) * jnp.exp2(TOP - power)
    return jnp.concatenate([scaled.reshape(-1, LANES), power]).astype(f16)


def decode(coded):
    value = coded.astype(f32)
    bound = jnp.exp2(value[-SUB:])
    scaled = value[:-SUB].reshape(-1, SUB, LANES) * (bound * 2.0**-TOP)
    return jnp.concatenate([scaled.reshape(-1, LANES), bound])


def largest(value):
    groups = [jnp.abs(value[rows]) for rows in spans(value.shape[0] // SUB, SUB)]
    return functools.reduce(jnp.maximum, groups)


def diagonal_kernel(bases, out):
    per_basis = bases.shape[1] // LANES
    columns = spans(per_basis, LANES)
    for at, (i, j) in zip(spans(len(own_tiles(per_basis)), LANES), own_tiles(per_basis)):
        out[at] = dot(bases[:, columns[i]], bases[:, columns[j]], TN)


def cross_kernel(at_ref, table, start, diagonal, *refs):
    n_batch = lax.axis_size("batch")
    pieces, (rows, message, *outs, both) = refs[: 2 * n_batch], refs[2 * n_batch :]
    chip, core, batch = at_ref[0], at_ref[1], at_ref[2]
    sub_rows, basis = pieces[0].shape
    for half in range(2):
        for offset in range(n_batch):
            first = pl.multiple_of(lax.bitwise_xor(batch, offset) * basis, basis)
            both[half * sub_rows : (half + 1) * sub_rows, pl.ds(first, basis)] = pieces[half * n_batch + offset][...]
    rows[...] = both[:sub_rows]
    index = 2 * chip + core
    share, size = start.shape[0] // lax.axis_size("rows"), start.shape[1]
    part = message.shape[0] - share * size // LANES - 2 * SUB
    message[:part] = diagonal[pl.ds(pl.multiple_of(index * part, SUB), part), :]
    message[part : part + SUB] = largest(message[:part])
    lower = part + SUB
    for k, lanes in enumerate(spans(size // LANES, LANES)):
        first = pl.multiple_of(index * share, SUB)
        message[lower + k * share : lower + (k + 1) * share] = start[pl.ds(first, share), lanes]
    message[lower + size // LANES * share :] = largest(message[lower : lower + size // LANES * share])
    for offset, out in enumerate(outs):
        share = out.shape[0] // LANES
        owner = 2 * lax.bitwise_xor(chip, offset) + core
        bound = jnp.zeros((SUB, LANES), f32)
        for j, at in enumerate(spans(share, LANES)):
            place = 2 * (owner * share + j)
            left = pl.multiple_of(table[place] * LANES, LANES)
            right = pl.multiple_of(table[place + 1] * LANES, LANES)
            tile = dot(both[:, pl.ds(left, LANES)], both[:, pl.ds(right, LANES)], TN)
            out[at] = tile
            bound = jnp.maximum(bound, largest(tile))
        out[share * LANES :] = bound


def spread(value, index):
    return jnp.broadcast_to(value[index : index + 1, :], value.shape)


def factor_block(work, background=()):
    background = list(background)
    groups = PANEL // SUB
    sub = lax.broadcasted_iota(jnp.int32, (SUB, LANES), 0)
    for r0 in range(0, LANES, PANEL):
        m = [
            [work[r0 + SUB * g : r0 + SUB * (g + 1), LANES * t : LANES * (t + 1)] for t in range(2)]
            for g in range(groups)
        ]
        col = {}
        scale = [None] * groups
        for j in range(PANEL):
            if j % STEP == 0:
                for k in range(j, j + STEP):
                    for g in range(k // SUB, groups):
                        col[k, g] = jnp.broadcast_to(m[g][0][:, r0 + k : r0 + k + 1], (SUB, LANES))
                pivot = spread(col[j, j // SUB], j % SUB)
            gj, sj = divmod(j, SUB)
            inverse = 1.0 / pivot
            root = lax.rsqrt(pivot)
            if (j + 1) % STEP:
                g, k = divmod(j + 1, SUB)
                entry = spread(col[j, g], k)
                pivot = spread(col[j + 1, g], k) - entry * entry * inverse
            if background and j % 8 == 4:
                background.pop(0)()
            scale[gj] = root if scale[gj] is None else jnp.where(sub == sj, root, scale[gj])
            source = [spread(m[gj][t], sj) for t in range(2)]
            scaled = {g: col[j, g] * inverse for g in range(gj, groups)}
            for k in range(j + 1, j - j % STEP + STEP):
                entry = spread(col[j, k // SUB], k % SUB)
                for g in range(k // SUB, groups):
                    col[k, g] = col[k, g] - scaled[g] * entry
            for g in range(gj, groups):
                factor = jnp.where(sub > sj, scaled[g], 0.0) if g == gj else scaled[g]
                for t in range(2):
                    m[g][t] = m[g][t] - factor * source[t]
        rows = jnp.concatenate(
            [jnp.concatenate([m[g][t] * scale[g] for t in range(2)], axis=1) for g in range(groups)], axis=0
        )
        work[r0 : r0 + PANEL, :] = rows
        below = r0 + PANEL
        if below < LANES:
            high, low = split(rows)
            left = jnp.concatenate([high[:, :LANES], high[:, :LANES], low[:, :LANES]], axis=0)
            right = jnp.concatenate([high, low, high], axis=0)
            work[below:, :] = work[below:, :] - dot(left, right, TN)[below:, :]


def identity(size):
    return lax.broadcasted_iota(jnp.int32, (size, size), 0) == lax.broadcasted_iota(jnp.int32, (size, size), 1)


def pair_of(ref, *at):
    return ref[0, *at], ref[1, *at]


def orthonormal_rows(a, rest, upper, work, out):
    size = a.shape[0]
    blocks = size // LANES
    lanes = lax.broadcasted_iota(jnp.int32, (LANES, size), 1)
    upper[...] = jnp.zeros(upper.shape, bf16)

    def block(k, carry):
        at = pl.ds(pl.multiple_of(k * LANES, LANES), LANES)
        last = pl.ds(pl.multiple_of(jnp.maximum(k - 1, 0) * LANES, LANES), LANES)
        following = pl.ds(pl.multiple_of(jnp.minimum(k + 1, blocks - 1) * LANES, LANES), LANES)
        work[:, :LANES] = a[at, at]
        work[:, LANES:] = identity(LANES).astype(f32)
        before = pair_of(upper)
        later = [jnp.where(lanes >= (k + 1) * LANES, part.astype(f32), 0.0).astype(bf16) for part in before]
        known = pair_of(out, last)

        def update(ref, rows, left, right):
            left = [part[:, rows] for part in left]
            ref[rows] = ref[rows] - dot_split(left, right, TN)

        background = [
            functools.partial(update, ref, rows, left, right)
            for ref, left, right in ((a, later, before), (rest, before, known))
            for rows in spans(blocks, LANES)
        ]
        factor_block(work, background)
        own = split(work[:, LANES:])
        rows = dot_split(own, split(a[at, :]), NN)
        upper[0], upper[1] = split(jnp.where(lanes >= (k + 1) * LANES, rows, 0.0))
        out[0, at], out[1, at] = split(dot_split(own, split(rest[at, :]), NN))
        a[following, :] = a[following, :] - dot_split(pair_of(upper, slice(None), following), pair_of(upper), TN)
        return carry

    lax.fori_loop(0, blocks, block, 0)


def prepare_kernel(at_ref, *refs):
    *blocks, high, low, diagonal, whole = refs
    chip, core, batch = at_ref[0], at_ref[1], at_ref[2]
    n_batch = blocks[0].shape[0]
    columns, size = whole.shape
    basis = columns // n_batch
    share = basis // len(blocks)
    part = diagonal.shape[1] // len(blocks)
    for k, block in enumerate(blocks):
        other, offset = divmod(k, len(blocks) // 2)
        row = 2 * lax.bitwise_xor(chip, offset) + lax.bitwise_xor(core, other)
        for z in range(n_batch):
            group = lax.bitwise_xor(batch, z)
            diagonal[group, pl.ds(pl.multiple_of(row * part, SUB), part), :] = block[z, :part, :]
            first = pl.multiple_of(group * basis + row * share, SUB)
            for k, lanes in enumerate(spans(size // LANES, LANES)):
                lower = part + SUB + k * share
                whole[pl.ds(first, share), lanes] = block[z, lower : lower + share, :]
    for rows in spans(columns // LANES, LANES):
        high[:, rows], low[:, rows] = split(whole[rows, :].T)


def trace_of(diagonal, per_basis):
    total = jnp.zeros((LANES, LANES), f32)
    eye = identity(LANES)
    for group in range(diagonal.shape[0]):
        for at, (i, j) in zip(spans(len(own_tiles(per_basis)), LANES), own_tiles(per_basis)):
            if i == j:
                total = total + jnp.where(eye, diagonal[group, at, :], 0.0)
    return jnp.sum(total)


def place_gram(at_ref, table, cross, diagonal, factor, pair):
    chip, core = at_ref[0], at_ref[1]
    devices, share_rows, _ = cross.shape
    share = share_rows // LANES
    n_batch = diagonal.shape[0]
    per_basis = pair[0].shape[0] // LANES // n_batch

    def place(k, carry):
        other, offset = k // (devices // 2), lax.rem(k, devices // 2)
        owner = 2 * lax.bitwise_xor(chip, offset) + lax.bitwise_xor(core, other)
        for j, inner in enumerate(spans(share, LANES)):
            at = 2 * (owner * share + j)
            row = pl.ds(pl.multiple_of(table[at] * LANES, LANES), LANES)
            column = pl.ds(pl.multiple_of(table[at + 1] * LANES, LANES), LANES)
            tile = cross[k, inner, :] * factor
            pair[0][row, column], pair[1][row, column] = split(tile)
            pair[0][column, row], pair[1][column, row] = split(tile.T)
        return carry

    lax.fori_loop(0, devices, place, 0)
    for group in range(n_batch):
        for at, (i, j) in zip(spans(len(own_tiles(per_basis)), LANES), own_tiles(per_basis)):
            rows, columns = (slice((group * per_basis + k) * LANES, (group * per_basis + k + 1) * LANES) for k in (i, j))
            for ref, value in zip(pair, split(diagonal[group, at, :] * factor)):
                ref[rows, columns] = value
                if i != j:
                    ref[columns, rows] = value.T


def solve_kernel(at_ref, table, cross, diagonal, sh, sl, rows, modes, ah, al, lifted, q, a, rest, upper, work):
    size, columns = sh.shape
    per_basis = columns // LANES // diagonal.shape[0]
    gram = (ah, al)
    factor = 1.0 / (trace_of(diagonal, per_basis) / columns)
    place_gram(at_ref, table, cross, diagonal, factor, gram)

    def lift(source, target):
        left = pair_of(source)

        def chunk(n, carry):
            at = pl.ds(pl.multiple_of(n * WIDE, WIDE), WIDE)
            before = source[0, :, at].astype(f32) + source[1, :, at].astype(f32)
            after = before + dot_split(left, (gram[0][:, at], gram[1][:, at]), NN)
            rest[:, at] = after
            target[0, :, at], target[1, :, at] = split(after)
            return carry

        lax.fori_loop(0, columns // WIDE, chunk, 0)

    def turn_of(step):
        return lax.rem(step + REPEAT - 1, REPEAT)

    def normalise(carry):
        step, failed = carry
        turn = turn_of(step)

        @pl.when(step < 2)
        def _():
            q[0], q[1] = sh[...], sl[...]

        @pl.when(step == 0)
        def _():
            lift(q, lifted)
            q[...] = lifted[...]

        @pl.when((step == 0) | (turn == 0))
        def _():
            lift(q, lifted)

        @pl.when((step != 0) & (turn != 0))
        def _():
            lifted[...] = q[...]
            rest[...] = q[0].astype(f32) + q[1].astype(f32)

        for at in spans(size // (2 * LANES), 2 * LANES):
            a[at, at.start :] = dot_split(pair_of(lifted, at), pair_of(lifted, slice(at.start, None)), NT)

        @pl.when((step != 0) & (turn < 2))
        def _():
            eye = identity(LANES)
            tiles = [a[at, at] for at in spans(size // LANES, LANES)]
            shift = SHIFT * jnp.sum(sum(jnp.where(eye, tile, 0.0) for tile in tiles))
            for at, tile in zip(spans(size // LANES, LANES), tiles):
                a[at, at] = tile + jnp.where(eye, shift, 0.0)

        orthonormal_rows(a, rest, upper, work, q)

        worst = jnp.zeros((LANES, 1), f32)
        for at in spans(size // LANES, LANES):
            gap = dot(q[0, at], q[0], NT)
            here = lax.broadcasted_iota(jnp.int32, gap.shape, 0) + at.start == lax.broadcasted_iota(jnp.int32, gap.shape, 1)
            gap = gap - here.astype(f32)
            worst = jnp.maximum(worst, jnp.sum(gap * gap, axis=1, keepdims=True))
        worst = jnp.max(worst)
        for at in spans(size // WIDE, WIDE):
            modes[:, at] = dot(rows[...], q[0, at], NT).astype(bf16)
        good = worst < ORTHO_TOL**2
        return step + 1, jnp.where((step == 0) & good, 0, failed)

    lax.while_loop(
        lambda carry: (carry[0] == 0) | ((carry[1] == 1) & (carry[0] <= ITERS * REPEAT)),
        normalise,
        (jnp.int32(0), jnp.int32(1)),
    )


def scratch_of(size, columns):
    return (
        [((columns, columns), bf16)] * 2
        + [((2, size, columns), bf16)] * 2
        + [((size, size), f32), ((size, columns), f32), ((2, LANES, size), bf16), ((LANES, 2 * LANES), f32)]
    )


def on_device(bases, start):
    local_rows, basis = bases.shape
    size = start.shape[1]
    n_batch, n_rows = lax.axis_size("batch"), lax.axis_size("rows")
    chips = n_rows // 2
    columns = basis * n_batch
    sub_rows = local_rows // n_batch
    per_basis = basis // LANES
    batch, row = lax.axis_index("batch"), lax.axis_index("rows")
    at = jnp.stack([row // 2, row % 2, batch]).astype(jnp.int32)
    tiles, share = tile_table(n_batch, per_basis, n_rows)
    table = jnp.asarray([k for tile in tiles for k in tile], jnp.int32)
    other_batches, other_chips = range(1, n_batch), range(2, n_rows, 2)

    def call(kernel, outs, scratch, *args, n_smem=0, flops=0, moved=1 << 20, after=()):
        def body(*refs):
            kernel(*refs[: len(args)], *refs[len(args) + len(after) :])

        held = [(a.shape, a.dtype) for a in args] + outs + scratch
        room = sum(math.prod(shape) * jnp.dtype(dtype).itemsize for shape, dtype in held)
        return pl.pallas_call(
            body,
            out_shape=[jax.ShapeDtypeStruct(shape, dtype) for shape, dtype in outs],
            in_specs=[SMEM] * n_smem + [VMEM] * (len(args) - n_smem) + [ANY] * len(after),
            out_specs=[VMEM] * len(outs),
            scratch_shapes=[pltpu.VMEM(shape, dtype) for shape, dtype in scratch],
            compiler_params=pltpu.CompilerParams(vmem_limit_bytes=(6 << 20) + room),
            cost_estimate=pl.CostEstimate(flops=flops, bytes_accessed=moved, transcendentals=0),
        )(*args, *after)

    pieces = []
    for offset in range(n_batch):
        piece = lax.dynamic_slice_in_dim(bases, (batch ^ offset) * sub_rows, sub_rows, 0)
        pieces.append(swap(piece, "batch", offset) if offset else piece)
    other_pieces = [swap(piece, "rows", 1) for piece in pieces]

    own_count = len(own_tiles(per_basis))
    (diagonal,) = call(
        diagonal_kernel, [((own_count * LANES, LANES), f32)], [], bases,
        flops=2 * local_rows * own_count * LANES * LANES, moved=bases.size * 2, after=other_pieces[:1],
    )
    diagonal = diagonal + swap(diagonal, "rows", 1)
    diagonal = sum((swap(diagonal, "rows", offset) for offset in other_chips), diagonal)

    part = own_count * LANES // n_rows
    message_rows = part + start.size // n_rows // LANES + 2 * SUB
    tile_rows = share * LANES
    rows, mine, *blocks = call(
        cross_kernel,
        [((sub_rows, columns), bf16), ((message_rows, LANES), f32)] + [((tile_rows + SUB, LANES), f32)] * chips,
        [((2 * sub_rows, columns), bf16)],
        at, table, start, diagonal, *pieces, *other_pieces, n_smem=2,
        flops=4 * sub_rows * chips * share * LANES * LANES, moved=6 << 20,
    )
    blocks = [encode(block) for block in blocks]
    blocks = blocks[:1] + [swap(block, "rows", offset) for block, offset in zip(blocks[1:], other_chips)]
    blocks[1], mine = lax.optimization_barrier((blocks[1], mine))
    plane = sum(decode(block) for block in blocks)
    planes = encode(plane)
    planes = [planes] + [swap(planes, "batch", offset) for offset in other_batches]
    total = encode(sum(decode(value) for value in planes))

    mine = jnp.concatenate([encode(mine[: part + SUB]), encode(mine[part + SUB :])])
    mine = spread_copy(mine, "batch", other_batches)
    mine = [mine] + [swap(mine, "rows", offset) for offset in other_chips]
    total, mine = lax.optimization_barrier((total, mine))

    def decode_message(blocks):
        return jnp.stack([jnp.concatenate([decode(b[: part + SUB]), decode(b[part + SUB :])]) for b in blocks])

    high, low, diagonal = call(
        prepare_kernel,
        [((size, columns), bf16)] * 2 + [((n_batch, own_count * LANES, LANES), f32)],
        [((columns, size), f32)],
        at, *map(decode_message, mine + [swap(block, "rows", 1) for block in mine]), n_smem=1, moved=8 << 20,
    )

    cross = spread_copy(total, "rows", other_chips)
    cross = jnp.concatenate([cross, swap(cross, "rows", 1)])
    cross = jax.vmap(decode)(cross)
    (modes,) = call(
        solve_kernel,
        [((sub_rows, size), bf16)],
        scratch_of(size, columns),
        at, table, cross, diagonal, high, low, rows, n_smem=2, flops=10**10, moved=10 << 20,
    )
    return modes


def solution(mesh):
    in_specs = (P("rows", "batch"), P("batch", None))
    out_specs = P(("rows", "batch"), None)
    return jax.shard_map(
        on_device, mesh=mesh, in_specs=in_specs, out_specs=out_specs, check_vma=False
    )
```

```python
import functools
import math

import jax
import jax.numpy as jnp
from jax import lax
from jax.experimental import pallas as pl
from jax.experimental.pallas import tpu as pltpu
from jax.sharding import PartitionSpec as P

ITERS = 2
LANES = 128
SUB = 8
PANEL = 32
STEP = 16
REPEAT = 4
SHIFT = 2.0**-15
WIDE = 512
ORTHO_TOL = 2.0**-8
NN = ((1,), (0,))
TN = ((0,), (0,))
NT = ((1,), (1,))
f32 = jnp.float32
bf16 = jnp.bfloat16
f16 = jnp.float16
TOP = 14.0
TINY = 2.0**-100
VMEM = pl.BlockSpec(memory_space=pltpu.VMEM)
ANY = pl.BlockSpec(memory_space=pl.ANY)
SMEM = pl.BlockSpec(memory_space=pltpu.SMEM)


def dot(left, right, dims):
    return lax.dot_general(left, right, (dims, ((), ())), preferred_element_type=f32)


def split(value):
    high = value.astype(bf16)
    return high, (value - high.astype(f32)).astype(bf16)


def dot_split(left, right, dims):
    (k_left,), (k_right,) = dims
    return dot(
        jnp.concatenate([left[0], left[0], left[1]], axis=k_left),
        jnp.concatenate([right[0], right[1], right[0]], axis=k_right),
        dims,
    )


def swap(value, axis, offset):
    size = lax.axis_size(axis)
    return lax.ppermute(value, axis, [(i, i ^ offset) for i in range(size)])


def spans(count, size):
    return [slice(i * size, (i + 1) * size) for i in range(count)]


def tile_table(n_batch, per_basis, n_rows):
    tiles = [
        (first * per_basis + i, second * per_basis + j)
        for first in range(n_batch)
        for second in range(first + 1, n_batch)
        for i in range(per_basis)
        for j in range(per_basis)
    ]
    share = -(-len(tiles) // n_rows)
    return tiles + tiles[-1:] * (share * n_rows - len(tiles)), share


def own_tiles(per_basis):
    return [(i, j) for i in range(per_basis) for j in range(i, per_basis)]


def spread_copy(value, axis, offsets):
    return jnp.stack([value] + [swap(value, axis, offset) for offset in offsets])


def encode(value):
    power = jnp.floor(jnp.log2(jnp.maximum(value[-SUB:], TINY))) + 1
    scaled = value[:-SUB].reshape(-1, SUB, LANES) * jnp.exp2(TOP - power)
    return jnp.concatenate([scaled.reshape(-1, LANES), power]).astype(f16)


def decode(coded):
    value = coded.astype(f32)
    bound = jnp.exp2(value[-SUB:])
    scaled = value[:-SUB].reshape(-1, SUB, LANES) * (bound * 2.0**-TOP)
    return jnp.concatenate([scaled.reshape(-1, LANES), bound])


def unscale(value, power):
    unit = jnp.exp2(power - TOP)
    return jnp.concatenate([value[rows] * unit for rows in spans(value.shape[0] // SUB, SUB)])


def largest(value):
    groups = [jnp.abs(value[rows]) for rows in spans(value.shape[0] // SUB, SUB)]
    return functools.reduce(jnp.maximum, groups)


def diagonal_kernel(bases, out):
    per_basis = bases.shape[1] // LANES
    columns = spans(per_basis, LANES)
    for at, (i, j) in zip(spans(len(own_tiles(per_basis)), LANES), own_tiles(per_basis)):
        out[at] = dot(bases[:, columns[i]], bases[:, columns[j]], TN)


def cross_kernel(at_ref, table, start, diagonal, *refs):
    n_batch = lax.axis_size("batch")
    pieces, (rows, message, *outs, both) = refs[: 2 * n_batch], refs[2 * n_batch :]
    chip, core, batch = at_ref[0], at_ref[1], at_ref[2]
    sub_rows, basis = pieces[0].shape
    for half in range(2):
        for offset in range(n_batch):
            first = pl.multiple_of(lax.bitwise_xor(batch, offset) * basis, basis)
            both[half * sub_rows : (half + 1) * sub_rows, pl.ds(first, basis)] = pieces[half * n_batch + offset][...]
    rows[...] = both[:sub_rows]
    index = 2 * chip + core
    share, size = start.shape[0] // lax.axis_size("rows"), start.shape[1]
    part = message.shape[0] - share * size // LANES - 2 * SUB
    message[:part] = diagonal[pl.ds(pl.multiple_of(index * part, SUB), part), :]
    message[part : part + SUB] = largest(message[:part])
    lower = part + SUB
    for k, lanes in enumerate(spans(size // LANES, LANES)):
        first = pl.multiple_of(index * share, SUB)
        message[lower + k * share : lower + (k + 1) * share] = start[pl.ds(first, share), lanes]
    message[lower + size // LANES * share :] = largest(message[lower : lower + size // LANES * share])
    for offset, out in enumerate(outs):
        share = out.shape[0] // LANES
        owner = 2 * lax.bitwise_xor(chip, offset) + core
        bound = jnp.zeros((SUB, LANES), f32)
        for j, at in enumerate(spans(share, LANES)):
            place = 2 * (owner * share + j)
            left = pl.multiple_of(table[place] * LANES, LANES)
            right = pl.multiple_of(table[place + 1] * LANES, LANES)
            tile = dot(both[:, pl.ds(left, LANES)], both[:, pl.ds(right, LANES)], TN)
            out[at] = tile
            bound = jnp.maximum(bound, largest(tile))
        out[share * LANES :] = bound


def spread(value, index):
    return jnp.broadcast_to(value[index : index + 1, :], value.shape)


def factor_block(work, background=()):
    background = list(background)
    groups = PANEL // SUB
    sub = lax.broadcasted_iota(jnp.int32, (SUB, LANES), 0)
    for r0 in range(0, LANES, PANEL):
        m = [
            [work[r0 + SUB * g : r0 + SUB * (g + 1), LANES * t : LANES * (t + 1)] for t in range(2)]
            for g in range(groups)
        ]
        col = {}
        scale = [None] * groups
        for j in range(PANEL):
            if j % STEP == 0:
                for k in range(j, j + STEP):
                    for g in range(k // SUB, groups):
                        col[k, g] = jnp.broadcast_to(m[g][0][:, r0 + k : r0 + k + 1], (SUB, LANES))
                pivot = spread(col[j, j // SUB], j % SUB)
            gj, sj = divmod(j, SUB)
            inverse = 1.0 / pivot
            root = lax.rsqrt(pivot)
            if (j + 1) % STEP:
                g, k = divmod(j + 1, SUB)
                entry = spread(col[j, g], k)
                pivot = spread(col[j + 1, g], k) - entry * entry * inverse
            if background and j % 8 == 4:
                background.pop(0)()
            scale[gj] = root if scale[gj] is None else jnp.where(sub == sj, root, scale[gj])
            source = [spread(m[gj][t], sj) for t in range(2)]
            scaled = {g: col[j, g] * inverse for g in range(gj, groups)}
            for k in range(j + 1, j - j % STEP + STEP):
                entry = spread(col[j, k // SUB], k % SUB)
                for g in range(k // SUB, groups):
                    col[k, g] = col[k, g] - scaled[g] * entry
            for g in range(gj, groups):
                factor = jnp.where(sub > sj, scaled[g], 0.0) if g == gj else scaled[g]
                for t in range(2):
                    m[g][t] = m[g][t] - factor * source[t]
        rows = jnp.concatenate(
            [jnp.concatenate([m[g][t] * scale[g] for t in range(2)], axis=1) for g in range(groups)], axis=0
        )
        work[r0 : r0 + PANEL, :] = rows
        below = r0 + PANEL
        if below < LANES:
            high, low = split(rows)
            left = jnp.concatenate([high[:, :LANES], high[:, :LANES], low[:, :LANES]], axis=0)
            right = jnp.concatenate([high, low, high], axis=0)
            work[below:, :] = work[below:, :] - dot(left, right, TN)[below:, :]


def identity(size):
    return lax.broadcasted_iota(jnp.int32, (size, size), 0) == lax.broadcasted_iota(jnp.int32, (size, size), 1)


def pair_of(ref, *at):
    return ref[0, *at], ref[1, *at]


def orthonormal_rows(a, rest, upper, work, out):
    size = a.shape[0]
    blocks = size // LANES
    lanes = lax.broadcasted_iota(jnp.int32, (LANES, size), 1)
    upper[...] = jnp.zeros(upper.shape, bf16)

    def block(k, carry):
        at = pl.ds(pl.multiple_of(k * LANES, LANES), LANES)
        last = pl.ds(pl.multiple_of(jnp.maximum(k - 1, 0) * LANES, LANES), LANES)
        following = pl.ds(pl.multiple_of(jnp.minimum(k + 1, blocks - 1) * LANES, LANES), LANES)
        work[:, :LANES] = a[at, at]
        work[:, LANES:] = identity(LANES).astype(f32)
        before = pair_of(upper)
        later = [jnp.where(lanes >= (k + 1) * LANES, part.astype(f32), 0.0).astype(bf16) for part in before]
        known = pair_of(out, last)

        def update(ref, rows, left, right):
            left = [part[:, rows] for part in left]
            ref[rows] = ref[rows] - dot_split(left, right, TN)

        background = [
            functools.partial(update, ref, rows, left, right)
            for ref, left, right in ((a, later, before), (rest, before, known))
            for rows in spans(blocks, LANES)
        ]
        factor_block(work, background)
        own = split(work[:, LANES:])
        rows = dot_split(own, split(a[at, :]), NN)
        upper[0], upper[1] = split(jnp.where(lanes >= (k + 1) * LANES, rows, 0.0))
        out[0, at], out[1, at] = split(dot_split(own, split(rest[at, :]), NN))
        a[following, :] = a[following, :] - dot_split(pair_of(upper, slice(None), following), pair_of(upper), TN)
        return carry

    lax.fori_loop(0, blocks, block, 0)


def prepare_kernel(at_ref, *refs):
    *blocks, high, low, diagonal, whole = refs
    chip, core, batch = at_ref[0], at_ref[1], at_ref[2]
    n_batch = blocks[0].shape[0]
    columns, size = whole.shape
    basis = columns // n_batch
    share = basis // len(blocks)
    part = diagonal.shape[1] // len(blocks)
    for k, block in enumerate(blocks):
        other, offset = divmod(k, len(blocks) // 2)
        row = 2 * lax.bitwise_xor(chip, offset) + lax.bitwise_xor(core, other)
        for z in range(n_batch):
            group = lax.bitwise_xor(batch, z)
            own = pl.ds(pl.multiple_of(row * part, SUB), part)
            diagonal[group, own, :] = unscale(block[z, :part, :], block[z, part : part + SUB, :])
            power = block[z, block.shape[1] - SUB :, :]
            first = pl.multiple_of(group * basis + row * share, SUB)
            for k, lanes in enumerate(spans(size // LANES, LANES)):
                lower = part + SUB + k * share
                whole[pl.ds(first, share), lanes] = unscale(block[z, lower : lower + share, :], power)
    for rows in spans(columns // LANES, LANES):
        high[:, rows], low[:, rows] = split(whole[rows, :].T)


def trace_of(diagonal, per_basis):
    total = jnp.zeros((LANES, LANES), f32)
    eye = identity(LANES)
    for group in range(diagonal.shape[0]):
        for at, (i, j) in zip(spans(len(own_tiles(per_basis)), LANES), own_tiles(per_basis)):
            if i == j:
                total = total + jnp.where(eye, diagonal[group, at, :], 0.0)
    return jnp.sum(total)


def place_gram(at_ref, table, cross, diagonal, factor, pair):
    chip, core = at_ref[0], at_ref[1]
    devices, share_rows, _ = cross.shape
    share = share_rows // LANES
    n_batch = diagonal.shape[0]
    per_basis = pair[0].shape[0] // LANES // n_batch

    def place(k, carry):
        other, offset = k // (devices // 2), lax.rem(k, devices // 2)
        owner = 2 * lax.bitwise_xor(chip, offset) + lax.bitwise_xor(core, other)
        for j, inner in enumerate(spans(share, LANES)):
            at = 2 * (owner * share + j)
            row = pl.ds(pl.multiple_of(table[at] * LANES, LANES), LANES)
            column = pl.ds(pl.multiple_of(table[at + 1] * LANES, LANES), LANES)
            tile = cross[k, inner, :] * factor
            pair[0][row, column], pair[1][row, column] = split(tile)
            pair[0][column, row], pair[1][column, row] = split(tile.T)
        return carry

    lax.fori_loop(0, devices, place, 0)
    for group in range(n_batch):
        for at, (i, j) in zip(spans(len(own_tiles(per_basis)), LANES), own_tiles(per_basis)):
            rows, columns = (slice((group * per_basis + k) * LANES, (group * per_basis + k + 1) * LANES) for k in (i, j))
            for ref, value in zip(pair, split(diagonal[group, at, :] * factor)):
                ref[rows, columns] = value
                if i != j:
                    ref[columns, rows] = value.T


def solve_kernel(at_ref, table, cross, diagonal, sh, sl, rows, modes, ah, al, lifted, q, a, rest, upper, work):
    size, columns = sh.shape
    per_basis = columns // LANES // diagonal.shape[0]
    gram = (ah, al)
    factor = 1.0 / (trace_of(diagonal, per_basis) / columns)
    place_gram(at_ref, table, cross, diagonal, factor, gram)

    def lift(source, target):
        left = pair_of(source)

        def chunk(n, carry):
            at = pl.ds(pl.multiple_of(n * WIDE, WIDE), WIDE)
            before = source[0, :, at].astype(f32) + source[1, :, at].astype(f32)
            after = before + dot_split(left, (gram[0][:, at], gram[1][:, at]), NN)
            rest[:, at] = after
            target[0, :, at], target[1, :, at] = split(after)
            return carry

        lax.fori_loop(0, columns // WIDE, chunk, 0)

    def turn_of(step):
        return lax.rem(step + REPEAT - 1, REPEAT)

    def normalise(carry):
        step, failed = carry
        turn = turn_of(step)

        @pl.when(step < 2)
        def _():
            q[0], q[1] = sh[...], sl[...]

        @pl.when(step == 0)
        def _():
            lift(q, lifted)
            q[...] = lifted[...]

        @pl.when((step == 0) | (turn == 0))
        def _():
            lift(q, lifted)

        @pl.when((step != 0) & (turn != 0))
        def _():
            lifted[...] = q[...]
            rest[...] = q[0].astype(f32) + q[1].astype(f32)

        for at in spans(size // (2 * LANES), 2 * LANES):
            a[at, at.start :] = dot_split(pair_of(lifted, at), pair_of(lifted, slice(at.start, None)), NT)

        @pl.when((step != 0) & (turn < 2))
        def _():
            eye = identity(LANES)
            tiles = [a[at, at] for at in spans(size // LANES, LANES)]
            shift = SHIFT * jnp.sum(sum(jnp.where(eye, tile, 0.0) for tile in tiles))
            for at, tile in zip(spans(size // LANES, LANES), tiles):
                a[at, at] = tile + jnp.where(eye, shift, 0.0)

        orthonormal_rows(a, rest, upper, work, q)

        worst = jnp.zeros((LANES, 1), f32)
        for at in spans(size // LANES, LANES):
            gap = dot(q[0, at], q[0], NT)
            here = lax.broadcasted_iota(jnp.int32, gap.shape, 0) + at.start == lax.broadcasted_iota(jnp.int32, gap.shape, 1)
            gap = gap - here.astype(f32)
            worst = jnp.maximum(worst, jnp.sum(gap * gap, axis=1, keepdims=True))
        worst = jnp.max(worst)
        for at in spans(size // WIDE, WIDE):
            modes[:, at] = dot(rows[...], q[0, at], NT).astype(bf16)
        good = worst < ORTHO_TOL**2
        return step + 1, jnp.where((step == 0) & good, 0, failed)

    lax.while_loop(
        lambda carry: (carry[0] == 0) | ((carry[1] == 1) & (carry[0] <= ITERS * REPEAT)),
        normalise,
        (jnp.int32(0), jnp.int32(1)),
    )


def scratch_of(size, columns):
    return (
        [((columns, columns), bf16)] * 2
        + [((2, size, columns), bf16)] * 2
        + [((size, size), f32), ((size, columns), f32), ((2, LANES, size), bf16), ((LANES, 2 * LANES), f32)]
    )


def on_device(bases, start):
    local_rows, basis = bases.shape
    size = start.shape[1]
    n_batch, n_rows = lax.axis_size("batch"), lax.axis_size("rows")
    chips = n_rows // 2
    columns = basis * n_batch
    sub_rows = local_rows // n_batch
    per_basis = basis // LANES
    batch, row = lax.axis_index("batch"), lax.axis_index("rows")
    at = jnp.stack([row // 2, row % 2, batch]).astype(jnp.int32)
    tiles, share = tile_table(n_batch, per_basis, n_rows)
    table = jnp.asarray([k for tile in tiles for k in tile], jnp.int32)
    other_batches, other_chips = range(1, n_batch), range(2, n_rows, 2)

    def call(kernel, outs, scratch, *args, n_smem=0, flops=0, moved=1 << 20, after=()):
        def body(*refs):
            kernel(*refs[: len(args)], *refs[len(args) + len(after) :])

        held = [(a.shape, a.dtype) for a in args] + outs + scratch
        room = sum(math.prod(shape) * jnp.dtype(dtype).itemsize for shape, dtype in held)
        return pl.pallas_call(
            body,
            out_shape=[jax.ShapeDtypeStruct(shape, dtype) for shape, dtype in outs],
            in_specs=[SMEM] * n_smem + [VMEM] * (len(args) - n_smem) + [ANY] * len(after),
            out_specs=[VMEM] * len(outs),
            scratch_shapes=[pltpu.VMEM(shape, dtype) for shape, dtype in scratch],
            compiler_params=pltpu.CompilerParams(vmem_limit_bytes=(6 << 20) + room),
            cost_estimate=pl.CostEstimate(flops=flops, bytes_accessed=moved, transcendentals=0),
        )(*args, *after)

    pieces = []
    for offset in range(n_batch):
        piece = lax.dynamic_slice_in_dim(bases, (batch ^ offset) * sub_rows, sub_rows, 0)
        pieces.append(swap(piece, "batch", offset) if offset else piece)
    other_pieces = [swap(piece, "rows", 1) for piece in pieces]

    own_count = len(own_tiles(per_basis))
    (diagonal,) = call(
        diagonal_kernel, [((own_count * LANES, LANES), f32)], [], bases,
        flops=2 * local_rows * own_count * LANES * LANES, moved=bases.size * 2, after=other_pieces[:1],
    )
    diagonal = diagonal + swap(diagonal, "rows", 1)
    diagonal = sum((swap(diagonal, "rows", offset) for offset in other_chips), diagonal)

    part = own_count * LANES // n_rows
    message_rows = part + start.size // n_rows // LANES + 2 * SUB
    tile_rows = share * LANES
    rows, mine, *blocks = call(
        cross_kernel,
        [((sub_rows, columns), bf16), ((message_rows, LANES), f32)] + [((tile_rows + SUB, LANES), f32)] * chips,
        [((2 * sub_rows, columns), bf16)],
        at, table, start, diagonal, *pieces, *other_pieces, n_smem=2,
        flops=4 * sub_rows * chips * share * LANES * LANES, moved=6 << 20,
    )
    blocks = [encode(block) for block in blocks]
    blocks = blocks[:1] + [swap(block, "rows", offset) for block, offset in zip(blocks[1:], other_chips)]
    blocks[1], mine = lax.optimization_barrier((blocks[1], mine))
    plane = sum(decode(block) for block in blocks)
    planes = encode(plane)
    planes = [planes] + [swap(planes, "batch", offset) for offset in other_batches]
    total = encode(sum(decode(value) for value in planes))

    mine = jnp.concatenate([encode(mine[: part + SUB]), encode(mine[part + SUB :])])
    mine = spread_copy(mine, "batch", other_batches)
    mine = [mine] + [swap(mine, "rows", offset) for offset in other_chips]
    total, mine = lax.optimization_barrier((total, mine))

    high, low, diagonal = call(
        prepare_kernel,
        [((size, columns), bf16)] * 2 + [((n_batch, own_count * LANES, LANES), f32)],
        [((columns, size), f32)],
        at, *(block.astype(f32) for block in mine + [swap(block, "rows", 1) for block in mine]),
        n_smem=1, moved=8 << 20,
    )

    cross = spread_copy(total, "rows", other_chips)
    cross = jnp.concatenate([cross, swap(cross, "rows", 1)])
    cross = jax.vmap(decode)(cross)
    (modes,) = call(
        solve_kernel,
        [((sub_rows, size), bf16)],
        scratch_of(size, columns),
        at, table, cross, diagonal, high, low, rows, n_smem=2, flops=10**10, moved=10 << 20,
    )
    return modes


def solution(mesh):
    in_specs = (P("rows", "batch"), P("batch", None))
    out_specs = P(("rows", "batch"), None)
    return jax.shard_map(
        on_device, mesh=mesh, in_specs=in_specs, out_specs=out_specs, check_vma=False
    )
```

```python
import functools
import math

import jax
import jax.numpy as jnp
from jax import lax
from jax.experimental import pallas as pl
from jax.experimental.pallas import tpu as pltpu
from jax.sharding import PartitionSpec as P

ITERS = 2
LANES = 128
SUB = 8
PANEL = 32
STEP = 16
REPEAT = 4
SHIFT = 2.0**-15
WIDE = 512
ORTHO_TOL = 2.0**-8
NN = ((1,), (0,))
TN = ((0,), (0,))
NT = ((1,), (1,))
f32 = jnp.float32
bf16 = jnp.bfloat16
f16 = jnp.float16
TOP = 14.0
TINY = 2.0**-100
VMEM = pl.BlockSpec(memory_space=pltpu.VMEM)
ANY = pl.BlockSpec(memory_space=pl.ANY)
SMEM = pl.BlockSpec(memory_space=pltpu.SMEM)


def dot(left, right, dims):
    return lax.dot_general(left, right, (dims, ((), ())), preferred_element_type=f32)


def split(value):
    high = value.astype(bf16)
    return high, (value - high.astype(f32)).astype(bf16)


def dot_split(left, right, dims):
    (k_left,), (k_right,) = dims
    return dot(
        jnp.concatenate([left[0], left[0], left[1]], axis=k_left),
        jnp.concatenate([right[0], right[1], right[0]], axis=k_right),
        dims,
    )


def swap(value, axis, offset):
    size = lax.axis_size(axis)
    return lax.ppermute(value, axis, [(i, i ^ offset) for i in range(size)])


def spans(count, size):
    return [slice(i * size, (i + 1) * size) for i in range(count)]


def tile_table(n_batch, per_basis, n_rows):
    tiles = [
        (first * per_basis + i, second * per_basis + j)
        for first in range(n_batch)
        for second in range(first + 1, n_batch)
        for i in range(per_basis)
        for j in range(per_basis)
    ]
    share = -(-len(tiles) // n_rows)
    return tiles + tiles[-1:] * (share * n_rows - len(tiles)), share


def own_tiles(per_basis):
    return [(i, j) for i in range(per_basis) for j in range(i, per_basis)]


def spread_copy(value, axis, offsets):
    return jnp.stack([value] + [swap(value, axis, offset) for offset in offsets])


def encode(value):
    power = jnp.floor(jnp.log2(jnp.maximum(value[-SUB:], TINY))) + 1
    scaled = value[:-SUB].reshape(-1, SUB, LANES) * jnp.exp2(TOP - power)
    return jnp.concatenate([scaled.reshape(-1, LANES), power]).astype(f16)


def decode(coded):
    value = coded.astype(f32)
    bound = jnp.exp2(value[-SUB:])
    scaled = value[:-SUB].reshape(-1, SUB, LANES) * (bound * 2.0**-TOP)
    return jnp.concatenate([scaled.reshape(-1, LANES), bound])


def unscale(value, power):
    unit = jnp.exp2(power - TOP)
    return jnp.concatenate([value[rows] * unit for rows in spans(value.shape[0] // SUB, SUB)])


def largest(value):
    groups = [jnp.abs(value[rows]) for rows in spans(value.shape[0] // SUB, SUB)]
    return functools.reduce(jnp.maximum, groups)


def diagonal_kernel(bases, out):
    per_basis = bases.shape[1] // LANES
    columns = spans(per_basis, LANES)
    for at, (i, j) in zip(spans(len(own_tiles(per_basis)), LANES), own_tiles(per_basis)):
        out[at] = dot(bases[:, columns[i]], bases[:, columns[j]], TN)


def cross_kernel(at_ref, table, start, diagonal, *refs):
    n_batch = lax.axis_size("batch")
    pieces, (rows, message, *outs, both) = refs[: 2 * n_batch], refs[2 * n_batch :]
    chip, core, batch = at_ref[0], at_ref[1], at_ref[2]
    sub_rows, basis = pieces[0].shape
    for half in range(2):
        for offset in range(n_batch):
            first = pl.multiple_of(lax.bitwise_xor(batch, offset) * basis, basis)
            both[half * sub_rows : (half + 1) * sub_rows, pl.ds(first, basis)] = pieces[half * n_batch + offset][...]
    rows[...] = both[:sub_rows]
    index = 2 * chip + core
    share, size = start.shape[0] // lax.axis_size("rows"), start.shape[1]
    part = message.shape[0] - share * size // LANES - 2 * SUB
    message[:part] = diagonal[pl.ds(pl.multiple_of(index * part, SUB), part), :]
    message[part : part + SUB] = largest(message[:part])
    lower = part + SUB
    for k, lanes in enumerate(spans(size // LANES, LANES)):
        first = pl.multiple_of(index * share, SUB)
        message[lower + k * share : lower + (k + 1) * share] = start[pl.ds(first, share), lanes]
    message[lower + size // LANES * share :] = largest(message[lower : lower + size // LANES * share])
    for offset, out in enumerate(outs):
        share = out.shape[0] // LANES
        owner = 2 * lax.bitwise_xor(chip, offset) + core
        bound = jnp.zeros((SUB, LANES), f32)
        for j, at in enumerate(spans(share, LANES)):
            place = 2 * (owner * share + j)
            left = pl.multiple_of(table[place] * LANES, LANES)
            right = pl.multiple_of(table[place + 1] * LANES, LANES)
            tile = dot(both[:, pl.ds(left, LANES)], both[:, pl.ds(right, LANES)], TN)
            out[at] = tile
            bound = jnp.maximum(bound, largest(tile))
        out[share * LANES :] = bound


def spread(value, index):
    return jnp.broadcast_to(value[index : index + 1, :], value.shape)


def factor_block(work, background=()):
    background = list(background)
    groups = PANEL // SUB
    sub = lax.broadcasted_iota(jnp.int32, (SUB, LANES), 0)
    for r0 in range(0, LANES, PANEL):
        m = [
            [work[r0 + SUB * g : r0 + SUB * (g + 1), LANES * t : LANES * (t + 1)] for t in range(2)]
            for g in range(groups)
        ]
        col = {}
        scale = [None] * groups
        for j in range(PANEL):
            if j % STEP == 0:
                for k in range(j, j + STEP):
                    for g in range(k // SUB, groups):
                        col[k, g] = jnp.broadcast_to(m[g][0][:, r0 + k : r0 + k + 1], (SUB, LANES))
                pivot = spread(col[j, j // SUB], j % SUB)
            gj, sj = divmod(j, SUB)
            inverse = 1.0 / pivot
            root = lax.rsqrt(pivot)
            if (j + 1) % STEP:
                g, k = divmod(j + 1, SUB)
                entry = spread(col[j, g], k)
                pivot = spread(col[j + 1, g], k) - entry * entry * inverse
            if background and j % 8 == 4:
                background.pop(0)()
            scale[gj] = root if scale[gj] is None else jnp.where(sub == sj, root, scale[gj])
            source = [spread(m[gj][t], sj) for t in range(2)]
            scaled = {g: col[j, g] * inverse for g in range(gj, groups)}
            for k in range(j + 1, j - j % STEP + STEP):
                entry = spread(col[j, k // SUB], k % SUB)
                for g in range(k // SUB, groups):
                    col[k, g] = col[k, g] - scaled[g] * entry
            for g in range(gj, groups):
                factor = jnp.where(sub > sj, scaled[g], 0.0) if g == gj else scaled[g]
                for t in range(2):
                    m[g][t] = m[g][t] - factor * source[t]
        rows = jnp.concatenate(
            [jnp.concatenate([m[g][t] * scale[g] for t in range(2)], axis=1) for g in range(groups)], axis=0
        )
        work[r0 : r0 + PANEL, :] = rows
        below = r0 + PANEL
        if below < LANES:
            high, low = split(rows)
            left = jnp.concatenate([high[:, :LANES], high[:, :LANES], low[:, :LANES]], axis=0)
            right = jnp.concatenate([high, low, high], axis=0)
            work[below:, :] = work[below:, :] - dot(left, right, TN)[below:, :]


def identity(size):
    return lax.broadcasted_iota(jnp.int32, (size, size), 0) == lax.broadcasted_iota(jnp.int32, (size, size), 1)


def pair_of(ref, *at):
    return ref[0, *at], ref[1, *at]


def orthonormal_rows(a, rest, upper, work, out):
    size = a.shape[0]
    blocks = size // LANES
    lanes = lax.broadcasted_iota(jnp.int32, (LANES, size), 1)
    upper[...] = jnp.zeros(upper.shape, bf16)

    def block(k, carry):
        at = pl.ds(pl.multiple_of(k * LANES, LANES), LANES)
        last = pl.ds(pl.multiple_of(jnp.maximum(k - 1, 0) * LANES, LANES), LANES)
        following = pl.ds(pl.multiple_of(jnp.minimum(k + 1, blocks - 1) * LANES, LANES), LANES)
        work[:, :LANES] = a[at, at]
        work[:, LANES:] = identity(LANES).astype(f32)
        before = pair_of(upper)
        later = [jnp.where(lanes >= (k + 1) * LANES, part.astype(f32), 0.0).astype(bf16) for part in before]
        known = pair_of(out, last)

        def update(ref, rows, left, right):
            left = [part[:, rows] for part in left]
            ref[rows] = ref[rows] - dot_split(left, right, TN)

        background = [
            functools.partial(update, ref, rows, left, right)
            for ref, left, right in ((a, later, before), (rest, before, known))
            for rows in spans(blocks, LANES)
        ]
        factor_block(work, background)
        own = split(work[:, LANES:])
        rows = dot_split(own, split(a[at, :]), NN)
        upper[0], upper[1] = split(jnp.where(lanes >= (k + 1) * LANES, rows, 0.0))
        out[0, at], out[1, at] = split(dot_split(own, split(rest[at, :]), NN))
        a[following, :] = a[following, :] - dot_split(pair_of(upper, slice(None), following), pair_of(upper), TN)
        return carry

    lax.fori_loop(0, blocks, block, 0)


def prepare_kernel(at_ref, *refs):
    *blocks, high, low, diagonal, whole = refs
    chip, core, batch = at_ref[0], at_ref[1], at_ref[2]
    n_batch = blocks[0].shape[0]
    columns, size = whole.shape
    basis = columns // n_batch
    share = basis // len(blocks)
    part = diagonal.shape[1] // len(blocks)
    for k, block in enumerate(blocks):
        other, offset = divmod(k, len(blocks) // 2)
        row = 2 * lax.bitwise_xor(chip, offset) + lax.bitwise_xor(core, other)
        for z in range(n_batch):
            group = lax.bitwise_xor(batch, z)
            own = pl.ds(pl.multiple_of(row * part, SUB), part)
            diagonal[group, own, :] = unscale(block[z, :part, :], block[z, part : part + SUB, :])
            power = block[z, block.shape[1] - SUB :, :]
            first = pl.multiple_of(group * basis + row * share, SUB)
            for k, lanes in enumerate(spans(size // LANES, LANES)):
                lower = part + SUB + k * share
                whole[pl.ds(first, share), lanes] = unscale(block[z, lower : lower + share, :], power)
    for rows in spans(columns // LANES, LANES):
        high[:, rows], low[:, rows] = split(whole[rows, :].T)


def trace_of(diagonal, per_basis):
    total = jnp.zeros((LANES, LANES), f32)
    eye = identity(LANES)
    for group in range(diagonal.shape[0]):
        for at, (i, j) in zip(spans(len(own_tiles(per_basis)), LANES), own_tiles(per_basis)):
            if i == j:
                total = total + jnp.where(eye, diagonal[group, at, :], 0.0)
    return jnp.sum(total)


def place_gram(at_ref, table, cross, diagonal, factor, pair):
    chip, core = at_ref[0], at_ref[1]
    devices, share_rows, _ = cross.shape
    share = share_rows // LANES
    n_batch = diagonal.shape[0]
    per_basis = pair[0].shape[0] // LANES // n_batch

    def place(k, carry):
        other, offset = k // (devices // 2), lax.rem(k, devices // 2)
        owner = 2 * lax.bitwise_xor(chip, offset) + lax.bitwise_xor(core, other)
        power = cross[k, share * LANES :, :]
        for j, inner in enumerate(spans(share, LANES)):
            at = 2 * (owner * share + j)
            row = pl.ds(pl.multiple_of(table[at] * LANES, LANES), LANES)
            column = pl.ds(pl.multiple_of(table[at + 1] * LANES, LANES), LANES)
            tile = unscale(cross[k, inner, :], power) * factor
            pair[0][row, column], pair[1][row, column] = split(tile)
            pair[0][column, row], pair[1][column, row] = split(tile.T)
        return carry

    lax.fori_loop(0, devices, place, 0, unroll=True)
    for group in range(n_batch):
        for at, (i, j) in zip(spans(len(own_tiles(per_basis)), LANES), own_tiles(per_basis)):
            rows, columns = (slice((group * per_basis + k) * LANES, (group * per_basis + k + 1) * LANES) for k in (i, j))
            for ref, value in zip(pair, split(diagonal[group, at, :] * factor)):
                ref[rows, columns] = value
                if i != j:
                    ref[columns, rows] = value.T


def solve_kernel(at_ref, table, cross, diagonal, sh, sl, rows, modes, ah, al, lifted, q, a, rest, upper, work):
    size, columns = sh.shape
    per_basis = columns // LANES // diagonal.shape[0]
    gram = (ah, al)
    factor = 1.0 / (trace_of(diagonal, per_basis) / columns)
    place_gram(at_ref, table, cross, diagonal, factor, gram)

    def lift(source, target):
        left = pair_of(source)

        def chunk(n, carry):
            at = pl.ds(pl.multiple_of(n * WIDE, WIDE), WIDE)
            before = source[0, :, at].astype(f32) + source[1, :, at].astype(f32)
            after = before + dot_split(left, (gram[0][:, at], gram[1][:, at]), NN)
            rest[:, at] = after
            target[0, :, at], target[1, :, at] = split(after)
            return carry

        lax.fori_loop(0, columns // WIDE, chunk, 0, unroll=True)

    def turn_of(step):
        return lax.rem(step + REPEAT - 1, REPEAT)

    def normalise(carry):
        step, failed = carry
        turn = turn_of(step)

        @pl.when(step < 2)
        def _():
            q[0], q[1] = sh[...], sl[...]

        @pl.when(step == 0)
        def _():
            lift(q, lifted)
            q[...] = lifted[...]

        @pl.when((step == 0) | (turn == 0))
        def _():
            lift(q, lifted)

        @pl.when((step != 0) & (turn != 0))
        def _():
            lifted[...] = q[...]
            rest[...] = q[0].astype(f32) + q[1].astype(f32)

        for at in spans(size // (2 * LANES), 2 * LANES):
            a[at, at.start :] = dot_split(pair_of(lifted, at), pair_of(lifted, slice(at.start, None)), NT)

        @pl.when((step != 0) & (turn < 2))
        def _():
            eye = identity(LANES)
            tiles = [a[at, at] for at in spans(size // LANES, LANES)]
            shift = SHIFT * jnp.sum(sum(jnp.where(eye, tile, 0.0) for tile in tiles))
            for at, tile in zip(spans(size // LANES, LANES), tiles):
                a[at, at] = tile + jnp.where(eye, shift, 0.0)

        orthonormal_rows(a, rest, upper, work, q)

        worst = jnp.zeros((LANES, 1), f32)
        for at in spans(size // LANES, LANES):
            gap = dot(q[0, at], q[0], NT)
            here = lax.broadcasted_iota(jnp.int32, gap.shape, 0) + at.start == lax.broadcasted_iota(jnp.int32, gap.shape, 1)
            gap = gap - here.astype(f32)
            worst = jnp.maximum(worst, jnp.sum(gap * gap, axis=1, keepdims=True))
        worst = jnp.max(worst)
        for at in spans(size // WIDE, WIDE):
            modes[:, at] = dot(rows[...], q[0, at], NT).astype(bf16)
        good = worst < ORTHO_TOL**2
        return step + 1, jnp.where((step == 0) & good, 0, failed)

    lax.while_loop(
        lambda carry: (carry[0] == 0) | ((carry[1] == 1) & (carry[0] <= ITERS * REPEAT)),
        normalise,
        (jnp.int32(0), jnp.int32(1)),
    )


def scratch_of(size, columns):
    return (
        [((columns, columns), bf16)] * 2
        + [((2, size, columns), bf16)] * 2
        + [((size, size), f32), ((size, columns), f32), ((2, LANES, size), bf16), ((LANES, 2 * LANES), f32)]
    )


def on_device(bases, start):
    local_rows, basis = bases.shape
    size = start.shape[1]
    n_batch, n_rows = lax.axis_size("batch"), lax.axis_size("rows")
    chips = n_rows // 2
    columns = basis * n_batch
    sub_rows = local_rows // n_batch
    per_basis = basis // LANES
    batch, row = lax.axis_index("batch"), lax.axis_index("rows")
    at = jnp.stack([row // 2, row % 2, batch]).astype(jnp.int32)
    tiles, share = tile_table(n_batch, per_basis, n_rows)
    table = jnp.asarray([k for tile in tiles for k in tile], jnp.int32)
    other_batches, other_chips = range(1, n_batch), range(2, n_rows, 2)

    def call(kernel, outs, scratch, *args, n_smem=0, flops=0, moved=1 << 20, after=()):
        def body(*refs):
            kernel(*refs[: len(args)], *refs[len(args) + len(after) :])

        held = [(a.shape, a.dtype) for a in args] + outs + scratch
        room = sum(math.prod(shape) * jnp.dtype(dtype).itemsize for shape, dtype in held)
        return pl.pallas_call(
            body,
            out_shape=[jax.ShapeDtypeStruct(shape, dtype) for shape, dtype in outs],
            in_specs=[SMEM] * n_smem + [VMEM] * (len(args) - n_smem) + [ANY] * len(after),
            out_specs=[VMEM] * len(outs),
            scratch_shapes=[pltpu.VMEM(shape, dtype) for shape, dtype in scratch],
            compiler_params=pltpu.CompilerParams(vmem_limit_bytes=(6 << 20) + room),
            cost_estimate=pl.CostEstimate(flops=flops, bytes_accessed=moved, transcendentals=0),
        )(*args, *after)

    pieces = []
    for offset in range(n_batch):
        piece = lax.dynamic_slice_in_dim(bases, (batch ^ offset) * sub_rows, sub_rows, 0)
        pieces.append(swap(piece, "batch", offset) if offset else piece)
    other_pieces = [swap(piece, "rows", 1) for piece in pieces]

    own_count = len(own_tiles(per_basis))
    (diagonal,) = call(
        diagonal_kernel, [((own_count * LANES, LANES), f32)], [], bases,
        flops=2 * local_rows * own_count * LANES * LANES, moved=bases.size * 2, after=other_pieces[:1],
    )
    diagonal = diagonal + swap(diagonal, "rows", 1)
    diagonal = sum((swap(diagonal, "rows", offset) for offset in other_chips), diagonal)

    part = own_count * LANES // n_rows
    message_rows = part + start.size // n_rows // LANES + 2 * SUB
    tile_rows = share * LANES
    rows, mine, *blocks = call(
        cross_kernel,
        [((sub_rows, columns), bf16), ((message_rows, LANES), f32)] + [((tile_rows + SUB, LANES), f32)] * chips,
        [((2 * sub_rows, columns), bf16)],
        at, table, start, diagonal, *pieces, *other_pieces, n_smem=2,
        flops=4 * sub_rows * chips * share * LANES * LANES, moved=6 << 20,
    )
    blocks = [encode(block) for block in blocks]
    blocks = blocks[:1] + [swap(block, "rows", offset) for block, offset in zip(blocks[1:], other_chips)]
    blocks[1], mine = lax.optimization_barrier((blocks[1], mine))
    plane = sum(decode(block) for block in blocks)
    planes = encode(plane)
    planes = [planes] + [swap(planes, "batch", offset) for offset in other_batches]
    total = encode(sum(decode(value) for value in planes))

    mine = jnp.concatenate([encode(mine[: part + SUB]), encode(mine[part + SUB :])])
    mine = spread_copy(mine, "batch", other_batches)
    mine = [mine] + [swap(mine, "rows", offset) for offset in other_chips]
    total, mine = lax.optimization_barrier((total, mine))

    high, low, diagonal = call(
        prepare_kernel,
        [((size, columns), bf16)] * 2 + [((n_batch, own_count * LANES, LANES), f32)],
        [((columns, size), f32)],
        at, *(block.astype(f32) for block in mine + [swap(block, "rows", 1) for block in mine]),
        n_smem=1, moved=8 << 20,
    )

    cross = spread_copy(total, "rows", other_chips)
    cross = jnp.concatenate([cross, swap(cross, "rows", 1)])
    cross = cross.astype(f32)
    (modes,) = call(
        solve_kernel,
        [((sub_rows, size), bf16)],
        scratch_of(size, columns),
        at, table, cross, diagonal, high, low, rows, n_smem=2, flops=10**10, moved=10 << 20,
    )
    return modes


def solution(mesh):
    in_specs = (P("rows", "batch"), P("batch", None))
    out_specs = P(("rows", "batch"), None)
    return jax.shard_map(
        on_device, mesh=mesh, in_specs=in_specs, out_specs=out_specs, check_vma=False
    )
```
